32 devices in a mesh: lon: 4 (over y, core), lat: 8 (over z, x).
Axes of the slice: x: 2, y: 2, z: 4, core: 2. Of those that a mesh axis runs over, the one named last changes fastest.
Arguments:
- fine_state: bfloat16 [512, 512, 128], P('lon', 'lat'), may hold values from -6 to 6
- coarse_state: bfloat16 [32, 32, 512], P('lon', 'lat'), may hold values from -6 to 6
- norm_gains: float32 [2, 128], replicated, may hold values from 0.25 to 1.75
- kernels: bfloat16 [2, 3, 3, 128, 128], replicated, may hold values from -0.1875 to 0.1875
- token_gain: float32 [512], replicated, may hold values from 0.25 to 1.75
- head_gains: float32 [2, 64], replicated, may hold values from 1.2 to 2.2
- query_weight: bfloat16 [512, 512], replicated, may hold values from -0.25 to 0.25
- keyvalue_weight: bfloat16 [512, 1024], replicated, may hold values from -0.25 to 0.25
- output_weight: bfloat16 [512, 512], replicated, may hold values from -0.25 to 0.25
- expand_weight: bfloat16 [512, 128], replicated, may hold values from -0.25 to 0.25
Outputs:
- fine_result: bfloat16 [512, 512, 128], P('lon', 'lat')
- coarse_result: bfloat16 [32, 32, 512], P('lon', 'lat')
The draws below stay inside these ranges and needn't reach their ends.
All inputs are finite; a program needn't handle non-finite values.
Results may differ from the reference program's by a relative error of at most 0.005.
Values may be sent and summed in bfloat16 or wider, within the bound.
A program may use at most 192 MiB of HBM per device.

```python
import math
import jax
import jax.numpy as jnp
from jax import lax

CH = 128
WIDTH = 512
HD = 64
HEADS = 8
PLON = 16
PLAT = 16
TDEV = 32
NLON = 512
NLAT = 512
GLON = 32
GLAT = 32
TOKENS = 1024


def level_of(stream_key, dims, pieces, low, largest):
    level = 1.0
    for axis_at, parts in pieces:
        steps = jax.random.uniform(jax.random.fold_in(jax.random.fold_in(stream_key, 6), axis_at), (parts,), jnp.float32, low / len(pieces), largest / len(pieces))
        level = level * jnp.repeat(jnp.exp(steps), dims[axis_at] // parts).reshape((-1,) + (1,) * (len(dims) - 1 - axis_at))
    return level


def scatter_about(key, dims, deviation, bound, cuts=(), dtype=jnp.bfloat16):
    values = jax.random.normal(key, dims, jnp.float32) * deviation
    if len(cuts) > 0:
        values = level_of(key, dims, cuts, -0.22, 0.18) * values
    return jnp.clip(values, min=-bound, max=bound).astype(dtype)


def setup_inputs(seed: int = 0) -> dict:
    seeds = jax.random.split(jax.random.key(seed), 11)
    fine_state = scatter_about(seeds[0], (NLON, NLAT, CH), 1.0, 6.0, ((0, 4), (1, 8)))
    coarse_state = scatter_about(seeds[1], (GLON, GLAT, WIDTH), 1.0, 6.0, ((0, 4), (1, 8)))
    norm_gains = jnp.clip(1.0 + 0.15 * jax.random.normal(seeds[2], (2, CH), jnp.float32), 0.25, 1.75)
    kernels = scatter_about(seeds[3], (2, 3, 3, CH, CH), (9 * CH) ** -0.5, 0.1875)
    token_gain = jnp.clip(1.0 + 0.15 * jax.random.normal(seeds[4], (WIDTH,), jnp.float32), 0.25, 1.75)
    head_gains = jnp.clip(jax.random.uniform(seeds[5], (2, HD), jnp.float32, 1.2, 2.2), 1.2, 2.2)
    query_weight = scatter_about(seeds[6], (WIDTH, WIDTH), WIDTH ** -0.5, 0.25)
    keyvalue_weight = scatter_about(seeds[7], (WIDTH, 2 * WIDTH), WIDTH ** -0.5, 0.25)
    output_weight = scatter_about(seeds[8], (WIDTH, WIDTH), WIDTH ** -0.5, 0.25)
    expand_weight = scatter_about(seeds[9], (WIDTH, CH), WIDTH ** -0.5, 0.25)
    return {"fine_state": fine_state, "coarse_state": coarse_state, "norm_gains": norm_gains, "kernels": kernels, "token_gain": token_gain, "head_gains": head_gains, "query_weight": query_weight, "keyvalue_weight": keyvalue_weight, "output_weight": output_weight, "expand_weight": expand_weight}


def rescale_rows(matrix, gain_row):
    return matrix * lax.rsqrt(lax.optimization_barrier(jnp.mean(matrix * matrix, axis=-1, keepdims=True)) + 1e-06) * gain_row

def rescale_heads(projected, gain_row):
    shaped = projected.reshape(projected.shape[0], HEADS, HD)
    return rescale_rows(shaped, gain_row)

def border_grid(hidden):
    wrapped = jnp.concatenate([hidden[-1:], hidden, hidden[:1]], axis=0)
    return jnp.pad(wrapped, ((0, 0), (1, 1), (0, 0)))

def convolve(padded, kernel):
    return lax.conv_general_dilated(padded[None], kernel, (1, 1), 'VALID', dimension_numbers=('NHWC', 'HWIO', 'NHWC'), preferred_element_type=jnp.float32)[0]

def reference(fine_state, coarse_state, norm_gains, kernels, token_gain, head_gains, query_weight, keyvalue_weight, output_weight, expand_weight):
    first_hidden = jax.nn.silu(rescale_rows(fine_state.astype(jnp.float32), norm_gains[0])).astype(jnp.bfloat16)
    first_output = convolve(border_grid(first_hidden), kernels[0])
    second_hidden = jax.nn.silu(rescale_rows(first_output, norm_gains[1])).astype(jnp.bfloat16)
    second_output = convolve(border_grid(second_hidden), kernels[1])
    tokens = coarse_state.reshape(TOKENS, WIDTH)
    normed = rescale_rows(tokens.astype(jnp.float32), token_gain).astype(jnp.bfloat16)
    scale_factor = 1.0 / math.sqrt(HD)
    queries = (rescale_heads(jnp.dot(normed, query_weight, preferred_element_type=jnp.float32), head_gains[0]) * scale_factor).astype(jnp.bfloat16)
    projected = jnp.dot(normed, keyvalue_weight, preferred_element_type=jnp.float32)
    key_rows = rescale_heads(projected[:, :WIDTH], head_gains[1]).astype(jnp.bfloat16)
    value_rows = projected[:, WIDTH:].astype(jnp.bfloat16).reshape(TOKENS, HEADS, HD)
    queries, key_rows, value_rows = lax.optimization_barrier((queries, key_rows, value_rows))
    key_wide = key_rows.astype(jnp.float32)
    value_wide = value_rows.astype(jnp.float32)

    def attend(query_block):
        scores = jnp.einsum('thd,shd->hts', query_block.astype(jnp.float32), key_wide)
        weights = jnp.exp(scores)
        totals = lax.optimization_barrier(jnp.sum(weights, axis=-1))
        rounded = lax.optimization_barrier(weights.astype(jnp.bfloat16)).astype(jnp.float32)
        summed = jnp.einsum('hts,shd->thd', rounded, value_wide)
        return (summed / jnp.transpose(totals)[:, :, None]).astype(jnp.bfloat16)
    query_blocks = queries.reshape(TOKENS // TDEV, TDEV, HEADS, HD)
    attended = lax.map(attend, query_blocks).reshape(TOKENS, WIDTH)
    coarse_result = (tokens.astype(jnp.float32) + jnp.dot(attended, output_weight, preferred_element_type=jnp.float32)).astype(jnp.bfloat16)
    lifted = jnp.dot(coarse_result, expand_weight, preferred_element_type=jnp.float32).reshape(GLON, 1, GLAT, 1, CH)
    merged = (fine_state.astype(jnp.float32) + second_output).reshape(GLON, PLON, GLAT, PLAT, CH) + lifted
    fine_result = merged.reshape(NLON, NLAT, CH).astype(jnp.bfloat16)
    return (fine_result, coarse_result.reshape(GLON, GLAT, WIDTH))
```

```python
import math

import jax
import jax.numpy as jnp
from jax import lax
from jax.sharding import PartitionSpec as P


def padded_2(block, sides, width, periodic):
    for axis, dim in sides:
        count = lax.axis_size(axis)
        forward = [(i, i + 1) for i in range(count - 1)]
        if periodic:
            forward.append((count - 1, 0))
        backward = [(target, source) for source, target in forward]
        low = lax.ppermute(
            lax.slice_in_dim(block, block.shape[dim] - width, None, axis=dim), axis, forward
        )
        high = lax.ppermute(lax.slice_in_dim(block, 0, width, axis=dim), axis, backward)
        block = jnp.concatenate([low, block, high], axis=dim)
    return block


def rescale_rows(matrix, gain_row):
    return matrix * lax.rsqrt(jnp.mean(matrix * matrix, axis=-1, keepdims=True) + 1e-06) * gain_row


def rescale_heads(projected, gain_row):
    shaped = projected.reshape(projected.shape[0], -1, gain_row.shape[0])
    return rescale_rows(shaped, gain_row)


def convolve(padded, kernel):
    return lax.conv_general_dilated(
        padded[None],
        kernel,
        (1, 1),
        "VALID",
        dimension_numbers=("NHWC", "HWIO", "NHWC"),
        preferred_element_type=jnp.float32,
    )[0]


def attach_rims(hidden, rim_width):
    wrapped = padded_2(hidden, (("lon", 0),), rim_width, True)
    return padded_2(wrapped, (("lat", 1),), rim_width, False)


def local(
    fine_state,
    coarse_state,
    norm_gains,
    kernels,
    token_gain,
    head_gains,
    query_weight,
    keyvalue_weight,
    output_weight,
    expand_weight,
):
    width_all = query_weight.shape[0]
    head_size = head_gains.shape[1]
    head_count = width_all // head_size
    lon_tokens = coarse_state.shape[0]
    lat_tokens = coarse_state.shape[1]
    lon_cells, lat_cells, channels = fine_state.shape
    first_hidden = jax.nn.silu(rescale_rows(fine_state.astype(jnp.float32), norm_gains[0])).astype(
        jnp.bfloat16
    )
    first_output = convolve(attach_rims(first_hidden, 1), kernels[0])
    second_hidden = jax.nn.silu(rescale_rows(first_output, norm_gains[1])).astype(jnp.bfloat16)
    second_output = convolve(attach_rims(second_hidden, 1), kernels[1])
    tokens = coarse_state.reshape(-1, width_all)
    normed = rescale_rows(tokens.astype(jnp.float32), token_gain).astype(jnp.bfloat16)
    scale_factor = 1.0 / math.sqrt(head_size)
    queries = (
        rescale_heads(
            jnp.dot(normed, query_weight, preferred_element_type=jnp.float32), head_gains[0]
        )
        * scale_factor
    ).astype(jnp.bfloat16)
    all_tokens = lax.all_gather(tokens, ("lon", "lat"), axis=0, tiled=True)
    all_normed = rescale_rows(all_tokens.astype(jnp.float32), token_gain).astype(jnp.bfloat16)
    projected = jnp.dot(all_normed, keyvalue_weight, preferred_element_type=jnp.float32)
    key_rows = (
        rescale_heads(projected[:, :width_all], head_gains[1])
        .astype(jnp.bfloat16)
        .reshape(-1, width_all)
    )
    value_rows = projected[:, width_all:].astype(jnp.bfloat16)
    accumulate_key_rows = key_rows
    accumulate_value_rows = value_rows
    key_heads = accumulate_key_rows.reshape(accumulate_key_rows.shape[0], head_count, head_size)
    value_heads = accumulate_value_rows.reshape(
        accumulate_value_rows.shape[0], head_count, head_size
    )
    scores = jnp.einsum("thd,shd->hts", queries, key_heads, preferred_element_type=jnp.float32)
    weights = jnp.exp(scores)
    totals = jnp.sum(weights, axis=-1)
    summed = jnp.einsum(
        "hts,shd->thd",
        weights.astype(jnp.bfloat16),
        value_heads,
        preferred_element_type=jnp.float32,
    )
    summed, totals = (summed, totals)
    attended = (
        (summed / jnp.transpose(totals)[:, :, None]).reshape(-1, width_all).astype(jnp.bfloat16)
    )
    coarse_result = (
        tokens.astype(jnp.float32)
        + jnp.dot(attended, output_weight, preferred_element_type=jnp.float32)
    ).astype(jnp.bfloat16)
    lifted = jnp.dot(coarse_result, expand_weight, preferred_element_type=jnp.float32).reshape(
        lon_tokens, 1, lat_tokens, 1, channels
    )
    merged = (fine_state.astype(jnp.float32) + second_output).reshape(
        lon_tokens, lon_cells // lon_tokens, lat_tokens, lat_cells // lat_tokens, channels
    ) + lifted
    fine_result = merged.reshape(lon_cells, lat_cells, channels).astype(jnp.bfloat16)
    return (fine_result, coarse_result.reshape(lon_tokens, lat_tokens, width_all))


def solution(mesh):
    return jax.shard_map(
        local,
        mesh=mesh,
        in_specs=(
            P("lon", "lat", None),
            P("lon", "lat", None),
            P(),
            P(),
            P(),
            P(),
            P(),
            P(),
            P(),
            P(),
        ),
        out_specs=(P("lon", "lat", None), P("lon", "lat", None)),
        check_vma=False,
    )
```

```python
import functools
import math

import jax
import jax.numpy as jnp
from jax import lax
from jax.experimental import pallas as pl
from jax.experimental.pallas import tpu as pltpu
from jax.sharding import PartitionSpec as P

MESH = pl.DeviceIdType.MESH
F32 = jnp.float32
BF16 = jnp.bfloat16
LEFT = 8


def mm(a, b):
    return jnp.dot(a, b, preferred_element_type=F32)


def block_ones(size, block, value):
    r = lax.broadcasted_iota(jnp.int32, (size, size), 0) // block
    c = lax.broadcasted_iota(jnp.int32, (size, size), 1) // block
    return jnp.where(r == c, value, 0.0).astype(BF16)


def silu(v):
    half = 0.5 * v
    return half + half * jnp.tanh(half)


def norm_silu(x, ones, gain):
    flat = x.reshape(-1, x.shape[-1])
    ms = mm((flat * flat).astype(BF16), ones)
    return silu(flat * lax.rsqrt(ms + 1e-6) * gain).reshape(x.shape)


def chunk_of(total, most):
    return max(d for d in range(1, most + 1) if total % d == 0)


def body(
    lon_n,
    lat_n,
    fine_hbm,
    coarse_hbm,
    norm_gains,
    kernels_hbm,
    token_gain,
    head_gains,
    wq_hbm,
    wkv_hbm,
    wo_hbm,
    we_hbm,
    out_hbm,
    coarse_out,
    fine,
    h1,
    h2,
    x,
    w,
    wq,
    wkv,
    wo,
    we,
    tok,
    lift,
    outs,
    halo,
    cols_s,
    cols_r,
    cols2_s,
    cols2_r,
    dma,
    wsem,
    osem,
    hs,
    hr,
    c2s,
    c2r,
    ts,
    tr,
):
    pairs, _, width, ch = fine.shape
    rows = 2 * pairs
    own, wide = coarse_hbm.shape
    lon, lat = lax.axis_index("lon"), lax.axis_index("lat")
    up, down = lax.rem(lon + lon_n - 1, lon_n), lax.rem(lon + 1, lon_n)
    west, east = lax.rem(lat + lat_n - 1, lat_n), lax.rem(lat + 1, lat_n)
    has_west, has_east = lat > 0, lat < lat_n - 1

    steps = []
    d = lat_n // 2
    while d:
        steps.append((lon, lat + d - 2 * d * ((lat // d) % 2)))
        d //= 2
    d = lon_n // 2
    while d:
        steps.append((lon + d - 2 * d * ((lon // d) % 2), lat))
        d //= 2

    local = [
        pltpu.make_async_copy(coarse_hbm, tok.at[pl.ds(0, own)], dma.at[0]),
        pltpu.make_async_copy(fine_hbm, fine, dma.at[1]),
        pltpu.make_async_copy(wq_hbm, wq, dma.at[2]),
        pltpu.make_async_copy(wkv_hbm, wkv, dma.at[3]),
        pltpu.make_async_copy(wo_hbm, wo, dma.at[4]),
        pltpu.make_async_copy(we_hbm, we, dma.at[5]),
    ]
    taps = []
    for conv in range(2):
        for r in range(2):
            for a in range(3):
                taps.append(
                    pltpu.make_async_copy(
                        kernels_hbm.at[conv, a],
                        w.at[conv, a + r, :, :, pl.ds(r * ch, ch)],
                        wsem.at[len(taps)],
                    )
                )
    local[0].start()
    local[1].start()
    for copy in taps:
        copy.start()
    for copy in local[2:]:
        copy.start()

    cols_r[...] = jnp.zeros_like(cols_r)
    cols2_r[...] = jnp.zeros_like(cols2_r)
    barrier = pltpu.get_barrier_semaphore()
    ring = [(i, j) for i in (up, lon, down) for j in (west, lat, east)]
    del ring[4]
    for device in ring + steps:
        pl.semaphore_signal(barrier, inc=1, device_id=device, device_id_type=MESH)

    zero = jnp.zeros((3, ch, ch), BF16)
    for conv in range(2):
        w[conv, 3, :, :, pl.ds(0, ch)] = zero
        w[conv, 0, :, :, pl.ds(ch, ch)] = zero
    ones = block_ones(ch, ch, 1.0 / ch)
    ones2 = block_ones(2 * ch, ch, 1.0 / ch)

    pl.semaphore_wait(barrier, len(ring) + len(steps))

    def step_copy(s):
        size = own << s
        return pltpu.make_async_remote_copy(
            src_ref=tok.at[pl.ds(0, size)],
            dst_ref=tok.at[pl.ds(size, size)],
            send_sem=ts.at[s],
            recv_sem=tr.at[s],
            device_id=steps[s],
            device_id_type=MESH,
        )

    state = {"at": 0}

    def advance():
        s = state["at"]
        if s < len(steps):
            step_copy(s).wait()
            if s + 1 < len(steps):
                step_copy(s + 1).start()
            state["at"] = s + 1

    local[0].wait()
    step_copy(0).start()

    def remote(src, dst, at, device):
        return pltpu.make_async_remote_copy(
            src_ref=src,
            dst_ref=dst,
            send_sem=hs.at[at],
            recv_sem=hr.at[at],
            device_id=device,
            device_id_type=MESH,
        )

    to_down = remote(fine_hbm.at[pl.ds(pairs - 1, 1)], halo.at[pl.ds(0, 1)], 0, (down, lat))
    to_up = remote(fine_hbm.at[pl.ds(0, 1)], halo.at[pl.ds(1, 1)], 1, (up, lat))
    to_down.start()
    to_up.start()

    local[1].wait()
    cols_s[0] = fine[:, :, 0:16, :].astype(F32)[:, :, 0:1, :]
    cols_s[1] = fine[:, :, width - 16 : width, :].astype(F32)[:, :, 15:16, :]
    side_copies = []
    for side, (there, ok_send) in enumerate(((west, has_west), (east, has_east))):
        got = cols_r.at[1 - side]
        mine = cols_s.at[side]
        side_copies.append(
            [
                remote(mine, got.at[pl.ds(1, pairs)], 2 + side * 3, (lon, there)),
                remote(
                    mine.at[pl.ds(pairs - 1, 1)],
                    got.at[pl.ds(0, 1)],
                    3 + side * 3,
                    (down, there),
                ),
                remote(
                    mine.at[pl.ds(0, 1)],
                    got.at[pl.ds(pairs + 1, 1)],
                    4 + side * 3,
                    (up, there),
                ),
            ]
        )

    def start_side(side):
        for copy in side_copies[side]:
            copy.start()

    pl.when(has_west)(lambda: start_side(0))
    pl.when(has_east)(lambda: start_side(1))

    gain0 = norm_gains[0:1, :]
    gain1 = norm_gains[1:2, :]
    n0 = chunk_of(pairs, 4)

    def first(i, c):
        at = pl.multiple_of(i * n0, n0)
        v = fine[pl.ds(at, n0)].astype(F32)
        h1[pl.ds(at + 1, n0), :, LEFT : LEFT + width, :] = norm_silu(v, ones, gain0)
        return c

    lax.fori_loop(0, pairs // n0, first, 0)
    advance()

    to_down.wait()
    to_up.wait()
    v = halo[...].astype(F32)
    v = norm_silu(v, ones, gain0)
    h1[0:1, :, LEFT : LEFT + width, :] = v[0:1]
    h1[pairs + 1 : pairs + 2, :, LEFT : LEFT + width, :] = v[1:2]

    def wait_send(side):
        for copy in side_copies[side]:
            copy.wait_send()

    def wait_recv(side):
        for copy in side_copies[side]:
            copy.wait_recv()

    pl.when(has_west)(lambda: wait_send(0))
    pl.when(has_east)(lambda: wait_send(1))
    pl.when(has_east)(lambda: wait_recv(0))
    pl.when(has_west)(lambda: wait_recv(1))
    gain0c = gain0.reshape(1, 1, 1, ch)
    for side, at in ((0, LEFT - 1), (1, LEFT + width)):
        v = cols_r[side]
        ms = jnp.mean(v * v, axis=-1, keepdims=True)
        h1[:, :, at : at + 1, :] = silu(v * lax.rsqrt(ms + 1e-6) * gain0c)

    def pack(src, count):
        n = chunk_of(count, 3)

        def go(i, c):
            at = i * n
            for q in range(2):
                for b in range(3):
                    lo = LEFT - 1 + b
                    col = (q * 3 + b) * ch
                    x[pl.ds(at, n), :, col : col + ch] = src[
                        pl.ds(at, n), q, lo : lo + width, :
                    ].astype(BF16)
            return c

        lax.fori_loop(0, count // n, go, 0)

    pack(h1, pairs + 2)
    advance()
    for copy in taps:
        copy.wait()

    half_k = 6 * ch

    def conv(at, n, conv_at):
        wa = w[conv_at, 0:2].reshape(half_k, 2 * ch)
        wb = w[conv_at, 2:4].reshape(half_k, 2 * ch)
        a = x[pl.ds(at, n)].reshape(n * width, half_k)
        b = x[pl.ds(at + 1, n)].reshape(n * width, half_k)
        return mm(a, wa) + mm(b, wb)

    n1 = chunk_of(pairs + 1, 5)

    def second(i, c):
        at = i * n1
        y = conv(at, n1, 0)
        ms = mm((y * y).astype(BF16), ones2)
        z = y * lax.rsqrt(ms + 1e-6)
        for q in range(2):
            v = silu(z[:, q * ch : (q + 1) * ch] * gain1)
            h2[pl.ds(at, n1), q, LEFT : LEFT + width, :] = v.reshape(n1, width, ch)
        return c

    loops = (pairs + 1) // n1
    lax.fori_loop(0, loops // 2, second, 0)
    advance()
    lax.fori_loop(loops // 2, loops, second, 0)
    advance()

    cols2_s[0] = h2[:, :, LEFT : LEFT + 1, :]
    cols2_s[1] = h2[:, :, LEFT + width - 1 : LEFT + width, :]

    def remote2(side, there):
        return pltpu.make_async_remote_copy(
            src_ref=cols2_s.at[side],
            dst_ref=cols2_r.at[1 - side],
            send_sem=c2s.at[side],
            recv_sem=c2r.at[side],
            device_id=(lon, there),
            device_id_type=MESH,
        )

    to_west, to_east = remote2(0, west), remote2(1, east)
    pl.when(has_west)(to_west.start)
    pl.when(has_east)(to_east.start)

    for copy in local[2:]:
        copy.wait()
    heads = wide // head_gains.shape[1]
    hd = wide // heads
    tg = token_gain[...]
    gq = jnp.concatenate([head_gains[0:1, :]] * heads, axis=1)
    gk = jnp.concatenate([head_gains[1:2, :]] * heads, axis=1)
    per_head = block_ones(wide, hd, 1.0 / hd)

    def norm_tokens(t):
        return (t * lax.rsqrt(jnp.mean(t * t, axis=-1, keepdims=True) + 1e-6) * tg).astype(BF16)

    def norm_heads(v, g):
        return v * lax.rsqrt(mm((v * v).astype(BF16), per_head) + 1e-6) * g

    mine = tok[0:own].astype(F32)
    q = norm_heads(mm(norm_tokens(mine), wq[...]), gq) * (1.0 / math.sqrt(hd))
    r = lax.broadcasted_iota(jnp.int32, (heads * own, wide), 0) // own
    c = lax.broadcasted_iota(jnp.int32, (heads * own, wide), 1) // hd
    head_mask = r == c
    qb = jnp.where(head_mask, jnp.concatenate([q] * heads, axis=0), 0.0).astype(BF16)
    while state["at"] < len(steps):
        advance()
    total = own * lon_n * lat_n
    nt = min(256, total)

    def attend(i, carry):
        acc, tot = carry
        t = tok[pl.ds(pl.multiple_of(i * nt, nt), nt)].astype(F32)
        kv = mm(norm_tokens(t), wkv[...])
        k = norm_heads(kv[:, :wide], gk).astype(BF16)
        vv = kv[:, wide:].astype(BF16)
        s = lax.dot_general(qb, k, (((1,), (1,)), ((), ())), preferred_element_type=F32)
        e = jnp.exp(s)
        return acc + mm(e.astype(BF16), vv), tot + jnp.sum(e, axis=1, keepdims=True)

    acc, tot = lax.fori_loop(
        0,
        total // nt,
        attend,
        (jnp.zeros((heads * own, wide), F32), jnp.zeros((heads * own, 1), F32)),
    )
    att = jnp.where(head_mask, acc / tot, 0.0).reshape(heads, own, wide)
    att = jnp.sum(att, axis=0).astype(BF16)
    coarse = (mine + mm(att, wo[...])).astype(BF16)
    coarse_out[...] = coarse
    lon_t = lift.shape[0]
    lat_t = own // lon_t
    rr = lax.broadcasted_iota(jnp.int32, (lon_t * width, own), 0) // (width // lat_t)
    cc = lax.broadcasted_iota(jnp.int32, (lon_t * width, own), 1)
    rep = mm(jnp.where(rr == cc, 1.0, 0.0).astype(BF16), coarse).astype(BF16)
    lift[...] = mm(rep, we[...]).reshape(lon_t, width, ch)

    pl.when(has_west)(to_west.wait_send)
    pl.when(has_east)(to_east.wait_send)
    pl.when(has_east)(to_west.wait_recv)
    pl.when(has_west)(to_east.wait_recv)
    h2[:, :, LEFT - 1 : LEFT, :] = cols2_r[0]
    h2[:, :, LEFT + width : LEFT + width + 1, :] = cols2_r[1]
    pack(h2, pairs + 1)
    n2 = pairs // lon_t

    def out_copy(i):
        at = pl.multiple_of(i * n2, n2)
        return pltpu.make_async_copy(
            outs.at[pl.ds(at, n2)], out_hbm.at[pl.ds(at, n2)], osem.at[i]
        )

    def third(i, c):
        at = pl.multiple_of(i * n2, n2)
        y = conv(at, n2, 1)
        up_row = lift[i]
        for q in range(2):
            v = y[:, q * ch : (q + 1) * ch].reshape(n2, width, ch)
            outs[pl.ds(at, n2), q] = (
                fine[pl.ds(at, n2), q].astype(F32) + v + up_row[None]
            ).astype(BF16)
        out_copy(i).start()
        return c

    lax.fori_loop(0, lon_t, third, 0)
    for i in range(lon_t):
        out_copy(i).wait()


def local(lon_n, lat_n, fine_state, coarse_state, norm_gains, kernels, token_gain, head_gains,
          query_weight, keyvalue_weight, output_weight, expand_weight):
    rows, width, ch = fine_state.shape
    lon_t, lat_t, wide = coarse_state.shape
    pairs, own = rows // 2, lon_t * lat_t
    hops = int(math.log2(lon_n)) + int(math.log2(lat_n))
    any_, vm = pl.BlockSpec(memory_space=pl.ANY), pl.BlockSpec(memory_space=pltpu.VMEM)
    sem = pltpu.SemaphoreType.DMA
    fine_result, coarse_result = pl.pallas_call(
        functools.partial(body, lon_n, lat_n),
        out_shape=(
            jax.ShapeDtypeStruct((pairs, 2, width, ch), BF16),
            jax.ShapeDtypeStruct((own, wide), BF16),
        ),
        in_specs=[any_, any_, vm, any_, vm, vm, any_, any_, any_, any_],
        out_specs=(any_, vm),
        scratch_shapes=[
            pltpu.VMEM((pairs, 2, width, ch), BF16),
            pltpu.VMEM((pairs + 2, 2, width + 16, ch), F32),
            pltpu.VMEM((pairs + 1, 2, width + 16, ch), F32),
            pltpu.VMEM((pairs + 2, width, 6 * ch), BF16),
            pltpu.VMEM((2, 4, 3, ch, 2 * ch), BF16),
            pltpu.VMEM(query_weight.shape, BF16),
            pltpu.VMEM(keyvalue_weight.shape, BF16),
            pltpu.VMEM(output_weight.shape, BF16),
            pltpu.VMEM(expand_weight.shape, BF16),
            pltpu.VMEM((own * lon_n * lat_n, wide), BF16),
            pltpu.VMEM((lon_t, width, ch), F32),
            pltpu.VMEM((pairs, 2, width, ch), BF16),
            pltpu.VMEM((2, 2, width, ch), BF16),
            pltpu.VMEM((2, pairs, 2, 1, ch), F32),
            pltpu.VMEM((2, pairs + 2, 2, 1, ch), F32),
            pltpu.VMEM((2, pairs + 1, 2, 1, ch), F32),
            pltpu.VMEM((2, pairs + 1, 2, 1, ch), F32),
            sem((6,)),
            sem((12,)),
            sem((lon_t,)),
            sem((8,)),
            sem((8,)),
            sem((2,)),
            sem((2,)),
            sem((hops,)),
            sem((hops,)),
        ],
        compiler_params=pltpu.CompilerParams(
            collective_id=0, has_side_effects=True, vmem_limit_bytes=56 * 2**20
        ),
    )(
        fine_state.reshape(pairs, 2, width, ch),
        coarse_state.reshape(own, wide),
        norm_gains,
        kernels,
        token_gain.reshape(1, wide),
        head_gains,
        query_weight,
        keyvalue_weight,
        output_weight,
        expand_weight,
    )
    return fine_result.reshape(fine_state.shape), coarse_result.reshape(coarse_state.shape)


def solution(mesh):
    split = P("lon", "lat", None)
    return jax.shard_map(
        functools.partial(local, mesh.shape["lon"], mesh.shape["lat"]),
        mesh=mesh,
        in_specs=(split, split) + (P(),) * 8,
        out_specs=(split, split),
        check_vma=False,
    )
```

```python
import functools
import math

import jax
import jax.numpy as jnp
from jax import lax
from jax.experimental import pallas as pl
from jax.experimental.pallas import tpu as pltpu
from jax.sharding import PartitionSpec as P

MESH = pl.DeviceIdType.MESH
F32 = jnp.float32
BF16 = jnp.bfloat16
LEFT = 8


def mm(a, b):
    return jnp.dot(a, b, preferred_element_type=F32)


def block_ones(size, block, value):
    r = lax.broadcasted_iota(jnp.int32, (size, size), 0) // block
    c = lax.broadcasted_iota(jnp.int32, (size, size), 1) // block
    return jnp.where(r == c, value, 0.0).astype(BF16)


def silu(v):
    half = 0.5 * v
    return half + half * jnp.tanh(half)


def norm_silu(x, ones, gain):
    flat = x.reshape(-1, x.shape[-1])
    ms = mm((flat * flat).astype(BF16), ones)
    return silu(flat * lax.rsqrt(ms + 1e-6) * gain).reshape(x.shape)


def chunk_of(total, most):
    return max(d for d in range(1, most + 1) if total % d == 0)


def body(
    lon_n,
    lat_n,
    fine_hbm,
    coarse_in,
    norm_gains,
    kernels_hbm,
    token_gain,
    head_gains,
    wq_hbm,
    wkv_hbm,
    wo_hbm,
    we_hbm,
    out_hbm,
    coarse_out,
    fine,
    hb,
    x1,
    x2,
    stage,
    w,
    wq,
    wkv,
    wo,
    we,
    tok,
    lift,
    outs,
    halo,
    cols_s,
    cols_r,
    cols2_s,
    cols2_r,
    dma,
    wsem,
    osem,
    hs,
    hr,
    c2s,
    c2r,
    ts,
    tr,
):
    pairs, _, width, ch = fine.shape
    rows = 2 * pairs
    lon_t, lat_t, wide = coarse_in.shape
    own = lon_t * lat_t
    lon, lat = lax.axis_index("lon"), lax.axis_index("lat")
    up, down = lax.rem(lon + lon_n - 1, lon_n), lax.rem(lon + 1, lon_n)
    west, east = lax.rem(lat + lat_n - 1, lat_n), lax.rem(lat + 1, lat_n)
    has_west, has_east = lat > 0, lat < lat_n - 1

    steps = []
    d = lat_n // 2
    while d:
        steps.append((lon, lat + d - 2 * d * ((lat // d) % 2)))
        d //= 2
    d = lon_n // 2
    while d:
        steps.append((lon + d - 2 * d * ((lon // d) % 2), lat))
        d //= 2

    local = [
        pltpu.make_async_copy(fine_hbm, fine, dma.at[0]),
        pltpu.make_async_copy(wq_hbm, wq, dma.at[1]),
        pltpu.make_async_copy(wkv_hbm, wkv, dma.at[2]),
        pltpu.make_async_copy(wo_hbm, wo, dma.at[3]),
        pltpu.make_async_copy(we_hbm, we, dma.at[4]),
    ]
    taps = []
    for conv in range(2):
        for r in range(2):
            for a in range(3):
                taps.append(
                    pltpu.make_async_copy(
                        kernels_hbm.at[conv, a],
                        w.at[conv, a + r, :, :, pl.ds(r * ch, ch)],
                        wsem.at[len(taps)],
                    )
                )
    for copy in local[:1] + taps + local[1:]:
        copy.start()

    cols_r[...] = jnp.zeros_like(cols_r)
    cols2_r[...] = jnp.zeros_like(cols2_r)
    hb[...] = jnp.zeros_like(hb)
    barrier = pltpu.get_barrier_semaphore()
    ring = [(i, j) for i in (up, lon, down) for j in (west, lat, east)]
    del ring[4]
    for device in ring + steps:
        pl.semaphore_signal(barrier, inc=1, device_id=device, device_id_type=MESH)

    for i in range(lon_t):
        stage[i * lat_t : (i + 1) * lat_t] = coarse_in[i].astype(F32)
    tok[0:own] = stage[...].astype(BF16)
    zero = jnp.zeros((3, ch, ch), BF16)
    for conv in range(2):
        w[conv, 3, :, :, pl.ds(0, ch)] = zero
        w[conv, 0, :, :, pl.ds(ch, ch)] = zero
    ones = block_ones(ch, ch, 1.0 / ch)
    ones2 = block_ones(2 * ch, ch, 1.0 / ch)

    pl.semaphore_wait(barrier, len(ring) + len(steps))

    def step_copy(s):
        size = own << s
        return pltpu.make_async_remote_copy(
            src_ref=tok.at[pl.ds(0, size)],
            dst_ref=tok.at[pl.ds(size, size)],
            send_sem=ts.at[s],
            recv_sem=tr.at[s],
            device_id=steps[s],
            device_id_type=MESH,
        )

    state = {"at": 0}

    def advance():
        s = state["at"]
        if s < len(steps):
            step_copy(s).wait()
            if s + 1 < len(steps):
                step_copy(s + 1).start()
            state["at"] = s + 1

    step_copy(0).start()

    def remote(src, dst, at, device):
        return pltpu.make_async_remote_copy(
            src_ref=src,
            dst_ref=dst,
            send_sem=hs.at[at],
            recv_sem=hr.at[at],
            device_id=device,
            device_id_type=MESH,
        )

    to_down = remote(fine_hbm.at[pl.ds(pairs - 1, 1)], halo.at[pl.ds(0, 1)], 0, (down, lat))
    to_up = remote(fine_hbm.at[pl.ds(0, 1)], halo.at[pl.ds(1, 1)], 1, (up, lat))
    to_down.start()
    to_up.start()

    local[0].wait()
    cols_s[0] = fine[:, :, 0:16, :].astype(F32)[:, :, 0:1, :]
    cols_s[1] = fine[:, :, width - 16 : width, :].astype(F32)[:, :, 15:16, :]
    side_copies = []
    for side, (there, ok_send) in enumerate(((west, has_west), (east, has_east))):
        got = cols_r.at[1 - side]
        mine = cols_s.at[side]
        side_copies.append(
            [
                remote(mine, got.at[pl.ds(1, pairs)], 2 + side * 3, (lon, there)),
                remote(
                    mine.at[pl.ds(pairs - 1, 1)],
                    got.at[pl.ds(0, 1)],
                    3 + side * 3,
                    (down, there),
                ),
                remote(
                    mine.at[pl.ds(0, 1)],
                    got.at[pl.ds(pairs + 1, 1)],
                    4 + side * 3,
                    (up, there),
                ),
            ]
        )

    def start_side(side):
        for copy in side_copies[side]:
            copy.start()

    pl.when(has_west)(lambda: start_side(0))
    pl.when(has_east)(lambda: start_side(1))

    gain0 = norm_gains[0:1, :]
    gain1 = norm_gains[1:2, :]
    n0 = chunk_of(pairs, 4)

    def put(dst, at, n, q, v, slot):
        base = q * 3 * ch
        room = hb.at[slot]
        room[0:n, q, LEFT : LEFT + width, :] = v
        dst[pl.ds(at, n), :, base + ch : base + 2 * ch] = v.astype(BF16)
        for b in (0, 2):
            lo = LEFT - 1 + b
            col = base + b * ch
            dst[pl.ds(at, n), :, col : col + ch] = room[0:n, q, lo : lo + width, :].astype(BF16)

    def patch(dst, cols):
        row = lax.broadcasted_iota(jnp.int32, (1, 16, ch), 1)
        for q in range(2):
            for side, lo, at in ((0, 0, 0), (1, width - 16, 15)):
                col = (q * 3 + 2 * side) * ch
                old = dst[:, lo : lo + 16, col : col + ch].astype(F32)
                new = jnp.where(row == at, cols[side][:, q], old)
                dst[:, lo : lo + 16, col : col + ch] = new.astype(BF16)

    def first(i, c):
        at = pl.multiple_of(i * n0, n0)
        v = norm_silu(fine[pl.ds(at, n0)].astype(F32), ones, gain0)
        for q in range(2):
            put(x1, at + 1, n0, q, v[:, q], q)
        return c

    loops = pairs // n0
    lax.fori_loop(0, loops // 2, first, 0)
    advance()
    lax.fori_loop(loops // 2, loops, first, 0)
    advance()

    to_down.wait()
    to_up.wait()
    v = norm_silu(halo[...].astype(F32), ones, gain0)
    for q in range(2):
        put(x1, 0, 1, q, v[0:1, q], 0)
        put(x1, pairs + 1, 1, q, v[1:2, q], 1)

    def wait_send(side):
        for copy in side_copies[side]:
            copy.wait_send()

    def wait_recv(side):
        for copy in side_copies[side]:
            copy.wait_recv()

    pl.when(has_west)(lambda: wait_send(0))
    pl.when(has_east)(lambda: wait_send(1))
    pl.when(has_east)(lambda: wait_recv(0))
    pl.when(has_west)(lambda: wait_recv(1))
    gain0c = gain0.reshape(1, 1, 1, ch)
    sides = []
    for side in range(2):
        v = cols_r[side]
        ms = jnp.mean(v * v, axis=-1, keepdims=True)
        sides.append(silu(v * lax.rsqrt(ms + 1e-6) * gain0c))
    patch(x1, sides)
    advance()
    for copy in taps:
        copy.wait()

    half_k = 6 * ch

    def conv(x, at, n, conv_at):
        wa = w[conv_at, 0:2].reshape(half_k, 2 * ch)
        wb = w[conv_at, 2:4].reshape(half_k, 2 * ch)
        a = x[pl.ds(at, n)].reshape(n * width, half_k)
        b = x[pl.ds(at + 1, n)].reshape(n * width, half_k)
        return mm(a, wa) + mm(b, wb)

    n1 = chunk_of(pairs + 1, 13)

    def second(i, c):
        at = i * n1
        parts = ((0, (n1 + 1) // 2), ((n1 + 1) // 2, n1))
        results = [conv(x1, at + lo, hi - lo, 0) for lo, hi in parts]
        for slot, (lo, hi) in enumerate(parts):
            y, n = results[slot], hi - lo
            ms = mm((y * y).astype(BF16), ones2)
            z = y * lax.rsqrt(ms + 1e-6)
            for q in range(2):
                v = silu(z[:, q * ch : (q + 1) * ch] * gain1).reshape(n, width, ch)
                put(x2, at + lo, n, q, v, slot)
                cols2_s[0, pl.ds(at + lo, n), q] = v[:, 0:1]
                cols2_s[1, pl.ds(at + lo, n), q] = v[:, width - 1 : width]
        return c

    loops = (pairs + 1) // n1
    lax.fori_loop(0, (loops + 1) // 2, second, 0)
    advance()
    lax.fori_loop((loops + 1) // 2, loops, second, 0)

    def remote2(side, there):
        return pltpu.make_async_remote_copy(
            src_ref=cols2_s.at[side],
            dst_ref=cols2_r.at[1 - side],
            send_sem=c2s.at[side],
            recv_sem=c2r.at[side],
            device_id=(lon, there),
            device_id_type=MESH,
        )

    to_west, to_east = remote2(0, west), remote2(1, east)
    pl.when(has_west)(to_west.start)
    pl.when(has_east)(to_east.start)

    for copy in local[1:]:
        copy.wait()
    heads = wide // head_gains.shape[1]
    hd = wide // heads
    tg = token_gain[...]
    gq = jnp.concatenate([head_gains[0:1, :]] * heads, axis=1)
    gk = jnp.concatenate([head_gains[1:2, :]] * heads, axis=1)
    per_head = block_ones(wide, hd, 1.0 / hd)

    def norm_tokens(t):
        return (t * lax.rsqrt(jnp.mean(t * t, axis=-1, keepdims=True) + 1e-6) * tg).astype(BF16)

    def norm_heads(v, g):
        return v * lax.rsqrt(mm((v * v).astype(BF16), per_head) + 1e-6) * g

    mine = stage[...]
    q = norm_heads(mm(norm_tokens(mine), wq[...]), gq) * (1.0 / math.sqrt(hd))
    r = lax.broadcasted_iota(jnp.int32, (heads * own, wide), 0) // own
    c = lax.broadcasted_iota(jnp.int32, (heads * own, wide), 1) // hd
    head_mask = r == c
    qb = jnp.where(head_mask, jnp.concatenate([q] * heads, axis=0), 0.0).astype(BF16)
    nt = 8 * own

    def attend(i, carry):
        acc, tot = carry
        t = tok[pl.ds(pl.multiple_of(i * nt, nt), nt)].astype(F32)
        kv = mm(norm_tokens(t), wkv[...])
        k = norm_heads(kv[:, :wide], gk).astype(BF16)
        vv = kv[:, wide:].astype(BF16)
        s = lax.dot_general(qb, k, (((1,), (1,)), ((), ())), preferred_element_type=F32)
        e = jnp.exp(s)
        return acc + mm(e.astype(BF16), vv), tot + jnp.sum(e, axis=1, keepdims=True)

    carry = (jnp.zeros((heads * own, wide), F32), jnp.zeros((heads * own, 1), F32))
    done = 0
    while done < lon_n * lat_n // 8:
        ready = (1 << state["at"]) // 8
        if ready > done:
            carry = lax.fori_loop(done, ready, attend, carry)
            done = ready
        advance()
    acc, tot = carry
    att = jnp.where(head_mask, acc / tot, 0.0).reshape(heads, own, wide)
    att = jnp.sum(att, axis=0).astype(BF16)
    coarse = (mine + mm(att, wo[...])).astype(BF16)
    stage[...] = coarse.astype(F32)
    for i in range(lon_t):
        coarse_out[i] = stage[i * lat_t : (i + 1) * lat_t].astype(BF16)
    rr = lax.broadcasted_iota(jnp.int32, (lon_t * width, own), 0) // (width // lat_t)
    cc = lax.broadcasted_iota(jnp.int32, (lon_t * width, own), 1)
    rep = mm(jnp.where(rr == cc, 1.0, 0.0).astype(BF16), coarse).astype(BF16)
    lift[...] = mm(rep, we[...]).reshape(lon_t, width, ch)

    pl.when(has_west)(to_west.wait_send)
    pl.when(has_east)(to_east.wait_send)
    pl.when(has_east)(to_west.wait_recv)
    pl.when(has_west)(to_east.wait_recv)
    patch(x2, cols2_r)
    n2 = pairs // lon_t

    def out_copy(i):
        at = pl.multiple_of(i * n2, n2)
        return pltpu.make_async_copy(
            outs.at[pl.ds(at, n2)], out_hbm.at[pl.ds(at, n2)], osem.at[i]
        )

    def third(i, c):
        results = [conv(x2, pl.multiple_of((2 * i + k) * n2, n2), n2, 1) for k in range(2)]
        for k in range(2):
            at = pl.multiple_of((2 * i + k) * n2, n2)
            y = results[k]
            up_row = lift[2 * i + k]
            for q in range(2):
                v = y[:, q * ch : (q + 1) * ch].reshape(n2, width, ch)
                outs[pl.ds(at, n2), q] = (
                    fine[pl.ds(at, n2), q].astype(F32) + v + up_row[None]
                ).astype(BF16)
            out_copy(2 * i + k).start()
        return c

    lax.fori_loop(0, lon_t // 2, third, 0)
    for i in range(lon_t):
        out_copy(i).wait()


def local(lon_n, lat_n, fine_state, coarse_state, norm_gains, kernels, token_gain, head_gains,
          query_weight, keyvalue_weight, output_weight, expand_weight):
    rows, width, ch = fine_state.shape
    lon_t, lat_t, wide = coarse_state.shape
    pairs, own = rows // 2, lon_t * lat_t
    hops = int(math.log2(lon_n)) + int(math.log2(lat_n))
    any_, vm = pl.BlockSpec(memory_space=pl.ANY), pl.BlockSpec(memory_space=pltpu.VMEM)
    sem = pltpu.SemaphoreType.DMA
    fine_result, coarse_result = pl.pallas_call(
        functools.partial(body, lon_n, lat_n),
        out_shape=(
            jax.ShapeDtypeStruct((pairs, 2, width, ch), BF16),
            jax.ShapeDtypeStruct(coarse_state.shape, BF16),
        ),
        in_specs=[any_, vm, vm, any_, vm, vm, any_, any_, any_, any_],
        out_specs=(any_, vm),
        scratch_shapes=[
            pltpu.VMEM((pairs, 2, width, ch), BF16),
            pltpu.VMEM((2, 7, 2, width + 16, ch), F32),
            pltpu.VMEM((pairs + 2, width, 6 * ch), BF16),
            pltpu.VMEM((pairs + 1, width, 6 * ch), BF16),
            pltpu.VMEM((own, wide), F32),
            pltpu.VMEM((2, 4, 3, ch, 2 * ch), BF16),
            pltpu.VMEM(query_weight.shape, BF16),
            pltpu.VMEM(keyvalue_weight.shape, BF16),
            pltpu.VMEM(output_weight.shape, BF16),
            pltpu.VMEM(expand_weight.shape, BF16),
            pltpu.VMEM((own * lon_n * lat_n, wide), BF16),
            pltpu.VMEM((lon_t, width, ch), F32),
            pltpu.VMEM((pairs, 2, width, ch), BF16),
            pltpu.VMEM((2, 2, width, ch), BF16),
            pltpu.VMEM((2, pairs, 2, 1, ch), F32),
            pltpu.VMEM((2, pairs + 2, 2, 1, ch), F32),
            pltpu.VMEM((2, pairs + 1, 2, 1, ch), F32),
            pltpu.VMEM((2, pairs + 1, 2, 1, ch), F32),
            sem((5,)),
            sem((12,)),
            sem((lon_t,)),
            sem((8,)),
            sem((8,)),
            sem((2,)),
            sem((2,)),
            sem((hops,)),
            sem((hops,)),
        ],
        compiler_params=pltpu.CompilerParams(
            collective_id=0, has_side_effects=True, vmem_limit_bytes=56 * 2**20
        ),
    )(
        fine_state.reshape(pairs, 2, width, ch),
        coarse_state,
        norm_gains,
        kernels,
        token_gain.reshape(1, wide),
        head_gains,
        query_weight,
        keyvalue_weight,
        output_weight,
        expand_weight,
    )
    return fine_result.reshape(fine_state.shape), coarse_result


def solution(mesh):
    split = P("lon", "lat", None)
    return jax.shard_map(
        functools.partial(local, mesh.shape["lon"], mesh.shape["lat"]),
        mesh=mesh,
        in_specs=(split, split) + (P(),) * 8,
        out_specs=(split, split),
        check_vma=False,
    )
```

```python
import functools
import math

import jax
import jax.numpy as jnp
from jax import lax
from jax.experimental import pallas as pl
from jax.experimental.pallas import tpu as pltpu
from jax.sharding import PartitionSpec as P

MESH = pl.DeviceIdType.MESH
F32 = jnp.float32
BF16 = jnp.bfloat16
LEFT = 8


def mm(a, b):
    return jnp.dot(a, b, preferred_element_type=F32)


def block_ones(size, block, value):
    r = lax.broadcasted_iota(jnp.int32, (size, size), 0) // block
    c = lax.broadcasted_iota(jnp.int32, (size, size), 1) // block
    return jnp.where(r == c, value, 0.0).astype(BF16)


def silu(v):
    half = 0.5 * v
    return half + half * jnp.tanh(half)


def norm_silu(x, ones, gain):
    flat = x.reshape(-1, x.shape[-1])
    ms = mm((flat * flat).astype(BF16), ones)
    return silu(flat * lax.rsqrt(ms + 1e-6) * gain).reshape(x.shape)


def chunk_of(total, most):
    return max(d for d in range(1, most + 1) if total % d == 0)


def body(
    lon_n,
    lat_n,
    fine,
    coarse_in,
    norm_gains,
    kernels,
    token_gain,
    head_gains,
    wq,
    wkv,
    wo,
    we,
    outs,
    coarse_out,
    hb,
    x1,
    x2,
    stage,
    w,
    tok,
    lift,
    halo,
    cols_s,
    cols_r,
    cols2_s,
    cols2_r,
    wsem,
    hs,
    hr,
    c2s,
    c2r,
    ts,
    tr,
):
    pairs, _, width, ch = fine.shape
    rows = 2 * pairs
    lon_t, lat_t, wide = coarse_in.shape
    own = lon_t * lat_t
    lon, lat = lax.axis_index("lon"), lax.axis_index("lat")
    up, down = lax.rem(lon + lon_n - 1, lon_n), lax.rem(lon + 1, lon_n)
    west, east = lax.rem(lat + lat_n - 1, lat_n), lax.rem(lat + 1, lat_n)
    has_west, has_east = lat > 0, lat < lat_n - 1

    by_z = ("lat", 2, lat_n // 2)
    by_x = ("lat", 1, 2)
    by_y = ("lon", 2, lon_n // 2)
    by_core = ("lon", 1, 2)
    chains = ((by_z, by_x, by_y, by_core), (by_z, by_y, by_x, by_core))

    def member(stage_at, offset):
        axis, stride, group = stage_at
        index = lon if axis == "lon" else lat
        place = (index // stride) % group
        moved = index + ((place + offset) % group - place) * stride
        return (moved, lat) if axis == "lon" else (lon, moved)

    partners = [member(stage_at, o) for stage_at in chains[0] for o in range(1, stage_at[2])]

    taps = []
    for conv in range(2):
        for r in range(2):
            for a in range(3):
                taps.append(
                    pltpu.make_async_copy(
                        kernels.at[conv, a],
                        w.at[conv, a + r, :, :, pl.ds(r * ch, ch)],
                        wsem.at[len(taps)],
                    )
                )
    for copy in taps:
        copy.start()

    cols_r[...] = jnp.zeros_like(cols_r)
    cols2_r[...] = jnp.zeros_like(cols2_r)
    hb[...] = jnp.zeros_like(hb)
    barrier = pltpu.get_barrier_semaphore()
    ring = [(i, j) for i in (up, lon, down) for j in (west, lat, east)]
    del ring[4]
    for device in ring + partners:
        pl.semaphore_signal(barrier, inc=1, device_id=device, device_id_type=MESH)

    for i in range(lon_t):
        stage[i * lat_t : (i + 1) * lat_t] = coarse_in[i].astype(F32)
    half_own = own // 2
    for half in range(2):
        tok[half, 0:half_own] = stage[half * half_own : (half + 1) * half_own].astype(BF16)
    zero = jnp.zeros((3, ch, ch), BF16)
    for conv in range(2):
        w[conv, 3, :, :, pl.ds(0, ch)] = zero
        w[conv, 0, :, :, pl.ds(ch, ch)] = zero
    ones = block_ones(ch, ch, 1.0 / ch)
    ones2 = block_ones(2 * ch, ch, 1.0 / ch)

    pl.semaphore_wait(barrier, len(ring) + len(partners))

    def stage_copies(level):
        copies = []
        for half in range(2):
            size, base = half_own, 0
            for done_stage in chains[half][:level]:
                size *= done_stage[2]
                base += done_stage[2] - 1
            for o in range(1, chains[half][level][2]):
                copies.append(
                    pltpu.make_async_remote_copy(
                        src_ref=tok.at[half, pl.ds(0, size)],
                        dst_ref=tok.at[half, pl.ds(o * size, size)],
                        send_sem=ts.at[half, base + o - 1],
                        recv_sem=tr.at[half, base + o - 1],
                        device_id=member(chains[half][level], o),
                        device_id_type=MESH,
                    )
                )
        return copies

    def held(level):
        return [half_own * math.prod(g[2] for g in chain[:level]) for chain in chains]

    state = {"at": 0}

    def start_stage(level):
        for copy in stage_copies(level):
            copy.start()

    def advance():
        level = state["at"]
        if level < 4:
            for copy in stage_copies(level):
                copy.wait()
            if level < 3:
                start_stage(level + 1)
            state["at"] = level + 1

    start_stage(0)

    def remote(src, dst, at, device):
        return pltpu.make_async_remote_copy(
            src_ref=src,
            dst_ref=dst,
            send_sem=hs.at[at],
            recv_sem=hr.at[at],
            device_id=device,
            device_id_type=MESH,
        )

    to_down = remote(fine.at[pl.ds(pairs - 1, 1)], halo.at[pl.ds(0, 1)], 0, (down, lat))
    to_up = remote(fine.at[pl.ds(0, 1)], halo.at[pl.ds(1, 1)], 1, (up, lat))
    to_down.start()
    to_up.start()

    cols_s[0] = fine[:, :, 0:16, :].astype(F32)[:, :, 0:1, :]
    cols_s[1] = fine[:, :, width - 16 : width, :].astype(F32)[:, :, 15:16, :]
    side_copies = []
    for side, (there, ok_send) in enumerate(((west, has_west), (east, has_east))):
        got = cols_r.at[1 - side]
        mine = cols_s.at[side]
        side_copies.append(
            [
                remote(mine, got.at[pl.ds(1, pairs)], 2 + side * 3, (lon, there)),
                remote(
                    mine.at[pl.ds(pairs - 1, 1)],
                    got.at[pl.ds(0, 1)],
                    3 + side * 3,
                    (down, there),
                ),
                remote(
                    mine.at[pl.ds(0, 1)],
                    got.at[pl.ds(pairs + 1, 1)],
                    4 + side * 3,
                    (up, there),
                ),
            ]
        )

    def start_side(side):
        for copy in side_copies[side]:
            copy.start()

    pl.when(has_west)(lambda: start_side(0))
    pl.when(has_east)(lambda: start_side(1))

    gain0 = norm_gains[0:1, :]
    gain1 = norm_gains[1:2, :]
    n0 = chunk_of(pairs, 4)

    def put(dst, at, n, q, v, slot):
        base = q * 3 * ch
        room = hb.at[slot]
        room[0:n, q, LEFT : LEFT + width, :] = v
        dst[pl.ds(at, n), :, base + ch : base + 2 * ch] = v.astype(BF16)
        for b in (0, 2):
            lo = LEFT - 1 + b
            col = base + b * ch
            dst[pl.ds(at, n), :, col : col + ch] = room[0:n, q, lo : lo + width, :].astype(BF16)

    def patch(dst, cols):
        row = lax.broadcasted_iota(jnp.int32, (1, 16, ch), 1)
        for q in range(2):
            for side, lo, at in ((0, 0, 0), (1, width - 16, 15)):
                col = (q * 3 + 2 * side) * ch
                old = dst[:, lo : lo + 16, col : col + ch].astype(F32)
                new = jnp.where(row == at, cols[side][:, q], old)
                dst[:, lo : lo + 16, col : col + ch] = new.astype(BF16)

    def first(i, c):
        at = pl.multiple_of(i * n0, n0)
        v = norm_silu(fine[pl.ds(at, n0)].astype(F32), ones, gain0)
        for q in range(2):
            put(x1, at + 1, n0, q, v[:, q], q)
        return c

    lax.fori_loop(0, pairs // n0, first, 0)

    to_down.wait()
    to_up.wait()
    v = norm_silu(halo[...].astype(F32), ones, gain0)
    for q in range(2):
        put(x1, 0, 1, q, v[0:1, q], 0)
        put(x1, pairs + 1, 1, q, v[1:2, q], 1)

    def wait_send(side):
        for copy in side_copies[side]:
            copy.wait_send()

    def wait_recv(side):
        for copy in side_copies[side]:
            copy.wait_recv()

    pl.when(has_west)(lambda: wait_send(0))
    pl.when(has_east)(lambda: wait_send(1))
    pl.when(has_east)(lambda: wait_recv(0))
    pl.when(has_west)(lambda: wait_recv(1))
    gain0c = gain0.reshape(1, 1, 1, ch)
    sides = []
    for side in range(2):
        v = cols_r[side]
        ms = jnp.mean(v * v, axis=-1, keepdims=True)
        sides.append(silu(v * lax.rsqrt(ms + 1e-6) * gain0c))
    patch(x1, sides)
    advance()
    for copy in taps:
        copy.wait()

    half_k = 6 * ch

    def conv(x, at, n, conv_at):
        wa = w[conv_at, 0:2].reshape(half_k, 2 * ch)
        wb = w[conv_at, 2:4].reshape(half_k, 2 * ch)
        a = x[pl.ds(at, n)].reshape(n * width, half_k)
        b = x[pl.ds(at + 1, n)].reshape(n * width, half_k)
        return mm(a, wa) + mm(b, wb)

    n1 = chunk_of(pairs + 1, 13)

    def second(i, c):
        at = i * n1
        parts = ((0, (n1 + 1) // 2), ((n1 + 1) // 2, n1))
        results = [conv(x1, at + lo, hi - lo, 0) for lo, hi in parts]
        for slot, (lo, hi) in enumerate(parts):
            y, n = results[slot], hi - lo
            ms = mm((y * y).astype(BF16), ones2)
            z = y * lax.rsqrt(ms + 1e-6)
            for q in range(2):
                v = silu(z[:, q * ch : (q + 1) * ch] * gain1).reshape(n, width, ch)
                put(x2, at + lo, n, q, v, slot)
                cols2_s[0, pl.ds(at + lo, n), q] = v[:, 0:1]
                cols2_s[1, pl.ds(at + lo, n), q] = v[:, width - 1 : width]
        return c

    loops = (pairs + 1) // n1
    lax.fori_loop(0, (loops + 1) // 2, second, 0)
    advance()
    lax.fori_loop((loops + 1) // 2, loops, second, 0)

    def remote2(side, there):
        return pltpu.make_async_remote_copy(
            src_ref=cols2_s.at[side],
            dst_ref=cols2_r.at[1 - side],
            send_sem=c2s.at[side],
            recv_sem=c2r.at[side],
            device_id=(lon, there),
            device_id_type=MESH,
        )

    to_west, to_east = remote2(0, west), remote2(1, east)
    pl.when(has_west)(to_west.start)
    pl.when(has_east)(to_east.start)

    heads = wide // head_gains.shape[1]
    hd = wide // heads
    tg = token_gain[...]
    gq = jnp.concatenate([head_gains[0:1, :]] * heads, axis=1)
    gk = jnp.concatenate([head_gains[1:2, :]] * heads, axis=1)
    per_head = block_ones(wide, hd, 1.0 / hd)

    def norm_tokens(t):
        return (t * lax.rsqrt(jnp.mean(t * t, axis=-1, keepdims=True) + 1e-6) * tg).astype(BF16)

    def norm_heads(v, g):
        return v * lax.rsqrt(mm((v * v).astype(BF16), per_head) + 1e-6) * g

    mine = stage[...]
    q = norm_heads(mm(norm_tokens(mine), wq[...]), gq) * (1.0 / math.sqrt(hd))
    r = lax.broadcasted_iota(jnp.int32, (heads * own, wide), 0) // own
    c = lax.broadcasted_iota(jnp.int32, (heads * own, wide), 1) // hd
    head_mask = r == c
    qb = jnp.where(head_mask, jnp.concatenate([q] * heads, axis=0), 0.0).astype(BF16)

    def attend(half, nt, i, carry):
        acc, tot = carry
        t = tok[half, pl.ds(pl.multiple_of(i * nt, nt), nt)].astype(F32)
        kv = mm(norm_tokens(t), wkv[...])
        k = norm_heads(kv[:, :wide], gk).astype(BF16)
        vv = kv[:, wide:].astype(BF16)
        s = lax.dot_general(qb, k, (((1,), (1,)), ((), ())), preferred_element_type=F32)
        e = jnp.exp(s)
        return acc + mm(e.astype(BF16), vv), tot + jnp.sum(e, axis=1, keepdims=True)

    carry = (jnp.zeros((heads * own, wide), F32), jnp.zeros((heads * own, 1), F32))
    done = [0, 0]
    while True:
        for half, ready in enumerate(held(state["at"])):
            more = ready - done[half]
            if more >= 128:
                nt = 256 if more % 256 == 0 and done[half] % 256 == 0 else 128
                carry = lax.fori_loop(
                    done[half] // nt, ready // nt, functools.partial(attend, half, nt), carry
                )
                done[half] = ready
        if state["at"] == 4:
            break
        advance()
    acc, tot = carry
    att = jnp.where(head_mask, acc / tot, 0.0).reshape(heads, own, wide)
    att = jnp.sum(att, axis=0).astype(BF16)
    coarse = (mine + mm(att, wo[...])).astype(BF16)
    stage[...] = coarse.astype(F32)
    for i in range(lon_t):
        coarse_out[i] = stage[i * lat_t : (i + 1) * lat_t].astype(BF16)
    rr = lax.broadcasted_iota(jnp.int32, (lon_t * width, own), 0) // (width // lat_t)
    cc = lax.broadcasted_iota(jnp.int32, (lon_t * width, own), 1)
    rep = mm(jnp.where(rr == cc, 1.0, 0.0).astype(BF16), coarse).astype(BF16)
    lift[...] = mm(rep, we[...]).reshape(lon_t, width, ch)

    pl.when(has_west)(to_west.wait_send)
    pl.when(has_east)(to_east.wait_send)
    pl.when(has_east)(to_west.wait_recv)
    pl.when(has_west)(to_east.wait_recv)
    patch(x2, cols2_r)
    n2 = pairs // lon_t

    def third(i, c):
        results = [conv(x2, pl.multiple_of((2 * i + k) * n2, n2), n2, 1) for k in range(2)]
        for k in range(2):
            at = pl.multiple_of((2 * i + k) * n2, n2)
            y = results[k]
            up_row = lift[2 * i + k]
            for q in range(2):
                v = y[:, q * ch : (q + 1) * ch].reshape(n2, width, ch)
                outs[pl.ds(at, n2), q] = (
                    fine[pl.ds(at, n2), q].astype(F32) + v + up_row[None]
                ).astype(BF16)
        return c

    lax.fori_loop(0, lon_t // 2, third, 0)


def local(lon_n, lat_n, fine_state, coarse_state, norm_gains, kernels, token_gain, head_gains,
          query_weight, keyvalue_weight, output_weight, expand_weight):
    rows, width, ch = fine_state.shape
    lon_t, lat_t, wide = coarse_state.shape
    pairs, own = rows // 2, lon_t * lat_t
    hops = lat_n // 2 + lon_n // 2
    tokens = own * lon_n * lat_n
    vm = pl.BlockSpec(memory_space=pltpu.VMEM)
    sem = pltpu.SemaphoreType.DMA
    fine_result, coarse_result = pl.pallas_call(
        functools.partial(body, lon_n, lat_n),
        out_shape=(
            jax.ShapeDtypeStruct((pairs, 2, width, ch), BF16),
            jax.ShapeDtypeStruct(coarse_state.shape, BF16),
        ),
        in_specs=[vm] * 10,
        out_specs=(vm, vm),
        scratch_shapes=[
            pltpu.VMEM((2, 7, 2, width + 16, ch), F32),
            pltpu.VMEM((pairs + 2, width, 6 * ch), BF16),
            pltpu.VMEM((pairs + 1, width, 6 * ch), BF16),
            pltpu.VMEM((own, wide), F32),
            pltpu.VMEM((2, 4, 3, ch, 2 * ch), BF16),
            pltpu.VMEM((2, tokens // 2, wide), BF16),
            pltpu.VMEM((lon_t, width, ch), F32),
            pltpu.VMEM((2, 2, width, ch), BF16),
            pltpu.VMEM((2, pairs, 2, 1, ch), F32),
            pltpu.VMEM((2, pairs + 2, 2, 1, ch), F32),
            pltpu.VMEM((2, pairs + 1, 2, 1, ch), F32),
            pltpu.VMEM((2, pairs + 1, 2, 1, ch), F32),
            sem((12,)),
            sem((8,)),
            sem((8,)),
            sem((2,)),
            sem((2,)),
            sem((2, hops)),
            sem((2, hops)),
        ],
        compiler_params=pltpu.CompilerParams(
            collective_id=0, has_side_effects=True, vmem_limit_bytes=36 * 2**20 + 2 * tokens * wide
        ),
    )(
        fine_state.reshape(pairs, 2, width, ch),
        coarse_state,
        norm_gains,
        kernels,
        token_gain.reshape(1, wide),
        head_gains,
        query_weight,
        keyvalue_weight,
        output_weight,
        expand_weight,
    )
    return fine_result.reshape(fine_state.shape), coarse_result


def solution(mesh):
    split = P("lon", "lat", None)
    return jax.shard_map(
        functools.partial(local, mesh.shape["lon"], mesh.shape["lat"]),
        mesh=mesh,
        in_specs=(split, split) + (P(),) * 8,
        out_specs=(split, split),
        check_vma=False,
    )
```

```python
import functools
import math

import jax
import jax.numpy as jnp
from jax import lax
from jax.experimental import pallas as pl
from jax.experimental.pallas import tpu as pltpu
from jax.sharding import PartitionSpec as P

MESH = pl.DeviceIdType.MESH
F32 = jnp.float32
BF16 = jnp.bfloat16
LEFT = 8


def mm(a, b):
    return jnp.dot(a, b, preferred_element_type=F32)


def block_ones(size, block, value):
    r = lax.broadcasted_iota(jnp.int32, (size, size), 0) // block
    c = lax.broadcasted_iota(jnp.int32, (size, size), 1) // block
    return jnp.where(r == c, value, 0.0).astype(BF16)


def silu(v):
    half = 0.5 * v
    return half + half * jnp.tanh(half)


def norm_silu(x, ones, gain):
    flat = x.reshape(-1, x.shape[-1])
    ms = mm((flat * flat).astype(BF16), ones)
    return silu(flat * lax.rsqrt(ms + 1e-6) * gain).reshape(x.shape)


def chunk_of(total, most):
    return max(d for d in range(1, most + 1) if total % d == 0)


def body(
    lon_n,
    lat_n,
    fine_hbm,
    coarse_in,
    norm_gains,
    kernels,
    token_gain,
    head_gains,
    wq_hbm,
    wkv_hbm,
    wo_hbm,
    we_hbm,
    out_hbm,
    coarse_out,
    outs,
    fine,
    wq,
    wkv,
    wo,
    we,
    hb,
    x1,
    x2,
    stage,
    w,
    tok,
    lift,
    halo,
    cols_s,
    cols_r,
    cols2_s,
    cols2_r,
    dma,
    wsem,
    osem,
    hs,
    hr,
    c2s,
    c2r,
    ts,
    tr,
):
    pairs, _, width, ch = fine.shape
    rows = 2 * pairs
    lon_t, lat_t, wide = coarse_in.shape
    own = lon_t * lat_t
    lon, lat = lax.axis_index("lon"), lax.axis_index("lat")
    up, down = lax.rem(lon + lon_n - 1, lon_n), lax.rem(lon + 1, lon_n)
    west, east = lax.rem(lat + lat_n - 1, lat_n), lax.rem(lat + 1, lat_n)
    has_west, has_east = lat > 0, lat < lat_n - 1

    by_z = ("lat", 2, lat_n // 2)
    by_x = ("lat", 1, 2)
    by_y = ("lon", 2, lon_n // 2)
    by_core = ("lon", 1, 2)
    chains = ((by_z, by_x, by_y, by_core), (by_z, by_y, by_x, by_core))

    def member(stage_at, offset):
        axis, stride, group = stage_at
        index = lon if axis == "lon" else lat
        place = (index // stride) % group
        moved = index + ((place + offset) % group - place) * stride
        return (moved, lat) if axis == "lon" else (lon, moved)

    partners = [member(stage_at, o) for stage_at in chains[0] for o in range(1, stage_at[2])]

    taps = []
    for conv in range(2):
        for r in range(2):
            for a in range(3):
                taps.append(
                    pltpu.make_async_copy(
                        kernels.at[conv, a],
                        w.at[conv, a + r, :, :, pl.ds(r * ch, ch)],
                        wsem.at[len(taps)],
                    )
                )
    local = [
        pltpu.make_async_copy(src, dst, dma.at[i])
        for i, (src, dst) in enumerate(
            ((fine_hbm, fine), (wq_hbm, wq), (wkv_hbm, wkv), (wo_hbm, wo), (we_hbm, we))
        )
    ]
    for copy in local[:1] + taps + local[1:]:
        copy.start()

    cols_r[...] = jnp.zeros_like(cols_r)
    cols2_r[...] = jnp.zeros_like(cols2_r)
    hb[...] = jnp.zeros_like(hb)
    barrier = pltpu.get_barrier_semaphore()
    ring = [(i, j) for i in (up, lon, down) for j in (west, lat, east)]
    del ring[4]
    for device in ring + partners:
        pl.semaphore_signal(barrier, inc=1, device_id=device, device_id_type=MESH)

    for i in range(lon_t):
        stage[i * lat_t : (i + 1) * lat_t] = coarse_in[i].astype(F32)
    half_own = own // 2
    for half in range(2):
        tok[half, 0:half_own] = stage[half * half_own : (half + 1) * half_own].astype(BF16)
    zero = jnp.zeros((3, ch, ch), BF16)
    for conv in range(2):
        w[conv, 3, :, :, pl.ds(0, ch)] = zero
        w[conv, 0, :, :, pl.ds(ch, ch)] = zero
    ones = block_ones(ch, ch, 1.0 / ch)
    ones2 = block_ones(2 * ch, ch, 1.0 / ch)

    pl.semaphore_wait(barrier, len(ring) + len(partners))

    def stage_copies(level):
        copies = []
        for half in range(2):
            size, base = half_own, 0
            for done_stage in chains[half][:level]:
                size *= done_stage[2]
                base += done_stage[2] - 1
            for o in range(1, chains[half][level][2]):
                copies.append(
                    pltpu.make_async_remote_copy(
                        src_ref=tok.at[half, pl.ds(0, size)],
                        dst_ref=tok.at[half, pl.ds(o * size, size)],
                        send_sem=ts.at[half, base + o - 1],
                        recv_sem=tr.at[half, base + o - 1],
                        device_id=member(chains[half][level], o),
                        device_id_type=MESH,
                    )
                )
        return copies

    def held(level):
        return [half_own * math.prod(g[2] for g in chain[:level]) for chain in chains]

    state = {"at": 0}

    def start_stage(level):
        for copy in stage_copies(level):
            copy.start()

    def advance():
        level = state["at"]
        if level < 4:
            for copy in stage_copies(level):
                copy.wait()
            if level < 3:
                start_stage(level + 1)
            state["at"] = level + 1

    start_stage(0)

    def remote(src, dst, at, device):
        return pltpu.make_async_remote_copy(
            src_ref=src,
            dst_ref=dst,
            send_sem=hs.at[at],
            recv_sem=hr.at[at],
            device_id=device,
            device_id_type=MESH,
        )

    to_down = remote(fine_hbm.at[pl.ds(pairs - 1, 1)], halo.at[pl.ds(0, 1)], 0, (down, lat))
    to_up = remote(fine_hbm.at[pl.ds(0, 1)], halo.at[pl.ds(1, 1)], 1, (up, lat))
    to_down.start()
    to_up.start()

    local[0].wait()
    cols_s[0] = fine[:, :, 0:16, :].astype(F32)[:, :, 0:1, :]
    cols_s[1] = fine[:, :, width - 16 : width, :].astype(F32)[:, :, 15:16, :]
    side_copies = []
    for side, (there, ok_send) in enumerate(((west, has_west), (east, has_east))):
        got = cols_r.at[1 - side]
        mine = cols_s.at[side]
        side_copies.append(
            [
                remote(mine, got.at[pl.ds(1, pairs)], 2 + side * 3, (lon, there)),
                remote(
                    mine.at[pl.ds(pairs - 1, 1)],
                    got.at[pl.ds(0, 1)],
                    3 + side * 3,
                    (down, there),
                ),
                remote(
                    mine.at[pl.ds(0, 1)],
                    got.at[pl.ds(pairs + 1, 1)],
                    4 + side * 3,
                    (up, there),
                ),
            ]
        )

    def start_side(side):
        for copy in side_copies[side]:
            copy.start()

    pl.when(has_west)(lambda: start_side(0))
    pl.when(has_east)(lambda: start_side(1))

    gain0 = norm_gains[0:1, :]
    gain1 = norm_gains[1:2, :]
    n0 = chunk_of(pairs, 4)

    def put(dst, at, n, q, v, slot):
        base = q * 3 * ch
        room = hb.at[slot]
        room[0:n, q, LEFT : LEFT + width, :] = v
        dst[pl.ds(at, n), :, base + ch : base + 2 * ch] = v.astype(BF16)
        for b in (0, 2):
            lo = LEFT - 1 + b
            col = base + b * ch
            dst[pl.ds(at, n), :, col : col + ch] = room[0:n, q, lo : lo + width, :].astype(BF16)

    def patch(dst, cols):
        row = lax.broadcasted_iota(jnp.int32, (1, 16, ch), 1)
        for q in range(2):
            for side, lo, at in ((0, 0, 0), (1, width - 16, 15)):
                col = (q * 3 + 2 * side) * ch
                old = dst[:, lo : lo + 16, col : col + ch].astype(F32)
                new = jnp.where(row == at, cols[side][:, q], old)
                dst[:, lo : lo + 16, col : col + ch] = new.astype(BF16)

    def first(i, c):
        at = pl.multiple_of(i * n0, n0)
        v = norm_silu(fine[pl.ds(at, n0)].astype(F32), ones, gain0)
        for q in range(2):
            put(x1, at + 1, n0, q, v[:, q], q)
        return c

    lax.fori_loop(0, pairs // n0, first, 0)

    to_down.wait()
    to_up.wait()
    v = norm_silu(halo[...].astype(F32), ones, gain0)
    for q in range(2):
        put(x1, 0, 1, q, v[0:1, q], 0)
        put(x1, pairs + 1, 1, q, v[1:2, q], 1)

    def wait_send(side):
        for copy in side_copies[side]:
            copy.wait_send()

    def wait_recv(side):
        for copy in side_copies[side]:
            copy.wait_recv()

    pl.when(has_west)(lambda: wait_send(0))
    pl.when(has_east)(lambda: wait_send(1))
    pl.when(has_east)(lambda: wait_recv(0))
    pl.when(has_west)(lambda: wait_recv(1))
    gain0c = gain0.reshape(1, 1, 1, ch)
    sides = []
    for side in range(2):
        v = cols_r[side]
        ms = jnp.mean(v * v, axis=-1, keepdims=True)
        sides.append(silu(v * lax.rsqrt(ms + 1e-6) * gain0c))
    patch(x1, sides)
    advance()
    for copy in taps:
        copy.wait()

    half_k = 6 * ch

    def conv(x, at, n, conv_at):
        wa = w[conv_at, 0:2].reshape(half_k, 2 * ch)
        wb = w[conv_at, 2:4].reshape(half_k, 2 * ch)
        a = x[pl.ds(at, n)].reshape(n * width, half_k)
        b = x[pl.ds(at + 1, n)].reshape(n * width, half_k)
        return mm(a, wa) + mm(b, wb)

    n1 = chunk_of(pairs + 1, 13)

    def second(i, c):
        at = i * n1
        parts = ((0, (n1 + 1) // 2), ((n1 + 1) // 2, n1))
        results = [conv(x1, at + lo, hi - lo, 0) for lo, hi in parts]
        for slot, (lo, hi) in enumerate(parts):
            y, n = results[slot], hi - lo
            ms = mm((y * y).astype(BF16), ones2)
            z = y * lax.rsqrt(ms + 1e-6)
            for q in range(2):
                v = silu(z[:, q * ch : (q + 1) * ch] * gain1).reshape(n, width, ch)
                put(x2, at + lo, n, q, v, slot)
                cols2_s[0, pl.ds(at + lo, n), q] = v[:, 0:1]
                cols2_s[1, pl.ds(at + lo, n), q] = v[:, width - 1 : width]
        return c

    loops = (pairs + 1) // n1
    lax.fori_loop(0, (loops + 1) // 2, second, 0)
    advance()
    lax.fori_loop((loops + 1) // 2, loops, second, 0)

    def remote2(side, there):
        return pltpu.make_async_remote_copy(
            src_ref=cols2_s.at[side],
            dst_ref=cols2_r.at[1 - side],
            send_sem=c2s.at[side],
            recv_sem=c2r.at[side],
            device_id=(lon, there),
            device_id_type=MESH,
        )

    to_west, to_east = remote2(0, west), remote2(1, east)
    pl.when(has_west)(to_west.start)
    pl.when(has_east)(to_east.start)

    for copy in local[1:]:
        copy.wait()
    heads = wide // head_gains.shape[1]
    hd = wide // heads
    tg = token_gain[...]
    gq = jnp.concatenate([head_gains[0:1, :]] * heads, axis=1)
    gk = jnp.concatenate([head_gains[1:2, :]] * heads, axis=1)
    per_head = block_ones(wide, hd, 1.0 / hd)

    def norm_tokens(t):
        return (t * lax.rsqrt(jnp.mean(t * t, axis=-1, keepdims=True) + 1e-6) * tg).astype(BF16)

    def norm_heads(v, g):
        return v * lax.rsqrt(mm((v * v).astype(BF16), per_head) + 1e-6) * g

    mine = stage[...]
    q = norm_heads(mm(norm_tokens(mine), wq[...]), gq) * (1.0 / math.sqrt(hd))
    r = lax.broadcasted_iota(jnp.int32, (heads * own, wide), 0) // own
    c = lax.broadcasted_iota(jnp.int32, (heads * own, wide), 1) // hd
    head_mask = r == c
    qb = jnp.where(head_mask, jnp.concatenate([q] * heads, axis=0), 0.0).astype(BF16)

    def attend(half, nt, i, carry):
        acc, tot = carry
        t = tok[half, pl.ds(pl.multiple_of(i * nt, nt), nt)].astype(F32)
        kv = mm(norm_tokens(t), wkv[...])
        k = norm_heads(kv[:, :wide], gk).astype(BF16)
        vv = kv[:, wide:].astype(BF16)
        s = lax.dot_general(qb, k, (((1,), (1,)), ((), ())), preferred_element_type=F32)
        e = jnp.exp(s)
        return acc + mm(e.astype(BF16), vv), tot + jnp.sum(e, axis=1, keepdims=True)

    carry = (jnp.zeros((heads * own, wide), F32), jnp.zeros((heads * own, 1), F32))
    done = [0, 0]
    while True:
        for half, ready in enumerate(held(state["at"])):
            more = ready - done[half]
            if more >= 128:
                nt = 256 if more % 256 == 0 and done[half] % 256 == 0 else 128
                carry = lax.fori_loop(
                    done[half] // nt, ready // nt, functools.partial(attend, half, nt), carry
                )
                done[half] = ready
        if state["at"] == 4:
            break
        advance()
    acc, tot = carry
    att = jnp.where(head_mask, acc / tot, 0.0).reshape(heads, own, wide)
    att = jnp.sum(att, axis=0).astype(BF16)
    coarse = (mine + mm(att, wo[...])).astype(BF16)
    stage[...] = coarse.astype(F32)
    for i in range(lon_t):
        coarse_out[i] = stage[i * lat_t : (i + 1) * lat_t].astype(BF16)
    rr = lax.broadcasted_iota(jnp.int32, (lon_t * width, own), 0) // (width // lat_t)
    cc = lax.broadcasted_iota(jnp.int32, (lon_t * width, own), 1)
    rep = mm(jnp.where(rr == cc, 1.0, 0.0).astype(BF16), coarse).astype(BF16)
    lift[...] = mm(rep, we[...]).reshape(lon_t, width, ch)

    pl.when(has_west)(to_west.wait_send)
    pl.when(has_east)(to_east.wait_send)
    pl.when(has_east)(to_west.wait_recv)
    pl.when(has_west)(to_east.wait_recv)
    patch(x2, cols2_r)
    n2 = pairs // lon_t

    def out_copy(i):
        at = pl.multiple_of(i * n2, n2)
        return pltpu.make_async_copy(
            outs.at[pl.ds(at, n2)], out_hbm.at[pl.ds(at, n2)], osem.at[i]
        )

    def third(i, c):
        results = [conv(x2, pl.multiple_of((2 * i + k) * n2, n2), n2, 1) for k in range(2)]
        for k in range(2):
            at = pl.multiple_of((2 * i + k) * n2, n2)
            y = results[k]
            up_row = lift[2 * i + k]
            for q in range(2):
                v = y[:, q * ch : (q + 1) * ch].reshape(n2, width, ch)
                outs[pl.ds(at, n2), q] = (
                    fine[pl.ds(at, n2), q].astype(F32) + v + up_row[None]
                ).astype(BF16)
            out_copy(2 * i + k).start()
        return c

    lax.fori_loop(0, lon_t // 2, third, 0)
    for i in range(lon_t):
        out_copy(i).wait()


def local(lon_n, lat_n, fine_state, coarse_state, norm_gains, kernels, token_gain, head_gains,
          query_weight, keyvalue_weight, output_weight, expand_weight):
    rows, width, ch = fine_state.shape
    lon_t, lat_t, wide = coarse_state.shape
    pairs, own = rows // 2, lon_t * lat_t
    hops = lat_n // 2 + lon_n // 2
    tokens = own * lon_n * lat_n
    vm = pl.BlockSpec(memory_space=pltpu.VMEM)
    hbm = pl.BlockSpec(memory_space=pltpu.HBM)
    sem = pltpu.SemaphoreType.DMA
    fine_result, coarse_result = pl.pallas_call(
        functools.partial(body, lon_n, lat_n),
        out_shape=(
            jax.ShapeDtypeStruct((pairs, 2, width, ch), BF16),
            jax.ShapeDtypeStruct(coarse_state.shape, BF16),
        ),
        in_specs=[hbm, vm, vm, hbm, vm, vm, hbm, hbm, hbm, hbm],
        out_specs=(hbm, vm),
        scratch_shapes=[
            pltpu.VMEM((pairs, 2, width, ch), BF16),
            pltpu.VMEM((pairs, 2, width, ch), BF16),
            pltpu.VMEM(query_weight.shape, BF16),
            pltpu.VMEM(keyvalue_weight.shape, BF16),
            pltpu.VMEM(output_weight.shape, BF16),
            pltpu.VMEM(expand_weight.shape, BF16),
            pltpu.VMEM((2, 7, 2, width + 16, ch), F32),
            pltpu.VMEM((pairs + 2, width, 6 * ch), BF16),
            pltpu.VMEM((pairs + 1, width, 6 * ch), BF16),
            pltpu.VMEM((own, wide), F32),
            pltpu.VMEM((2, 4, 3, ch, 2 * ch), BF16),
            pltpu.VMEM((2, tokens // 2, wide), BF16),
            pltpu.VMEM((lon_t, width, ch), F32),
            pltpu.VMEM((2, 2, width, ch), BF16),
            pltpu.VMEM((2, pairs, 2, 1, ch), F32),
            pltpu.VMEM((2, pairs + 2, 2, 1, ch), F32),
            pltpu.VMEM((2, pairs + 1, 2, 1, ch), F32),
            pltpu.VMEM((2, pairs + 1, 2, 1, ch), F32),
            sem((5,)),
            sem((12,)),
            sem((lon_t,)),
            sem((8,)),
            sem((8,)),
            sem((2,)),
            sem((2,)),
            sem((2, hops)),
            sem((2, hops)),
        ],
        compiler_params=pltpu.CompilerParams(
            collective_id=0, has_side_effects=True, vmem_limit_bytes=56 * 2**20
        ),
    )(
        fine_state.reshape(pairs, 2, width, ch),
        coarse_state,
        norm_gains,
        kernels,
        token_gain.reshape(1, wide),
        head_gains,
        query_weight,
        keyvalue_weight,
        output_weight,
        expand_weight,
    )
    return fine_result.reshape(fine_state.shape), coarse_result


def solution(mesh):
    split = P("lon", "lat", None)
    return jax.shard_map(
        functools.partial(local, mesh.shape["lon"], mesh.shape["lat"]),
        mesh=mesh,
        in_specs=(split, split) + (P(),) * 8,
        out_specs=(split, split),
        check_vma=False,
    )
```

```python
import functools
import math

import jax
import jax.numpy as jnp
from jax import lax
from jax.experimental import pallas as pl
from jax.experimental.pallas import tpu as pltpu
from jax.sharding import PartitionSpec as P

MESH = pl.DeviceIdType.MESH
F32 = jnp.float32
BF16 = jnp.bfloat16
LEFT = 8


def mm(a, b):
    return jnp.dot(a, b, preferred_element_type=F32)


def block_ones(size, block, value):
    r = lax.broadcasted_iota(jnp.int32, (size, size), 0) // block
    c = lax.broadcasted_iota(jnp.int32, (size, size), 1) // block
    return jnp.where(r == c, value, 0.0).astype(BF16)


def silu(v):
    half = 0.5 * v
    return half + half * jnp.tanh(half)


def norm_silu(x, ones, gain):
    flat = x.reshape(-1, x.shape[-1])
    ms = mm((flat * flat).astype(BF16), ones)
    return silu(flat * lax.rsqrt(ms + 1e-6) * gain).reshape(x.shape)


def chunk_of(total, most):
    return max(d for d in range(1, most + 1) if total % d == 0)


def body(
    lon_n,
    lat_n,
    fine_hbm,
    coarse_in,
    norm_gains,
    kernels,
    token_gain,
    head_gains,
    wq_hbm,
    wkv_hbm,
    wo_hbm,
    we_hbm,
    out_hbm,
    coarse_out,
    outs,
    fine,
    wq,
    wkv,
    wo,
    we,
    hb,
    x1,
    x2,
    stage,
    w,
    tok,
    lift,
    halo,
    cols_s,
    cols_r,
    cols2_s,
    cols2_r,
    dma,
    wsem,
    osem,
    hs,
    hr,
    c2s,
    c2r,
    ts,
    tr,
):
    pairs, _, width, ch = fine.shape
    rows = 2 * pairs
    lon_t, lat_t, wide = coarse_in.shape
    own = lon_t * lat_t
    lon, lat = lax.axis_index("lon"), lax.axis_index("lat")
    up, down = lax.rem(lon + lon_n - 1, lon_n), lax.rem(lon + 1, lon_n)
    west, east = lax.rem(lat + lat_n - 1, lat_n), lax.rem(lat + 1, lat_n)
    has_west, has_east = lat > 0, lat < lat_n - 1

    by_z = ("lat", 2, lat_n // 2)
    by_x = ("lat", 1, 2)
    by_y = ("lon", 2, lon_n // 2)
    by_core = ("lon", 1, 2)
    chains = ((by_z, by_x, by_y, by_core), (by_z, by_y, by_x, by_core))

    def member(stage_at, offset):
        axis, stride, group = stage_at
        index = lon if axis == "lon" else lat
        place = (index // stride) % group
        moved = index + ((place + offset) % group - place) * stride
        return (moved, lat) if axis == "lon" else (lon, moved)

    partners = [member(stage_at, o) for stage_at in chains[0] for o in range(1, stage_at[2])]

    taps = []
    for conv in range(2):
        for r in range(2):
            for a in range(3):
                taps.append(
                    pltpu.make_async_copy(
                        kernels.at[conv, a],
                        w.at[conv, a + r, :, :, pl.ds(r * ch, ch)],
                        wsem.at[len(taps)],
                    )
                )
    local = [
        pltpu.make_async_copy(src, dst, dma.at[i])
        for i, (src, dst) in enumerate(
            ((fine_hbm, fine), (wq_hbm, wq), (wkv_hbm, wkv), (wo_hbm, wo), (we_hbm, we))
        )
    ]
    for copy in local[:1] + taps + local[1:]:
        copy.start()

    cols_r[...] = jnp.zeros_like(cols_r)
    cols2_r[...] = jnp.zeros_like(cols2_r)
    hb[...] = jnp.zeros_like(hb)
    barrier = pltpu.get_barrier_semaphore()
    ring = [(i, j) for i in (up, lon, down) for j in (west, lat, east)]
    del ring[4]
    for device in ring + partners:
        pl.semaphore_signal(barrier, inc=1, device_id=device, device_id_type=MESH)

    for i in range(lon_t):
        stage[i * lat_t : (i + 1) * lat_t] = coarse_in[i].astype(F32)
    half_own = own // 2
    for half in range(2):
        tok[half, 0:half_own] = stage[half * half_own : (half + 1) * half_own].astype(BF16)
    zero = jnp.zeros((3, ch, ch), BF16)
    for conv in range(2):
        w[conv, 3, :, :, pl.ds(0, ch)] = zero
        w[conv, 0, :, :, pl.ds(ch, ch)] = zero
    ones = block_ones(ch, ch, 1.0 / ch)
    ones2 = block_ones(2 * ch, ch, 1.0 / ch)

    pl.semaphore_wait(barrier, len(ring) + len(partners))

    def stage_copies(level):
        copies = []
        for half in range(2):
            size, base = half_own, 0
            for done_stage in chains[half][:level]:
                size *= done_stage[2]
                base += done_stage[2] - 1
            for o in range(1, chains[half][level][2]):
                copies.append(
                    pltpu.make_async_remote_copy(
                        src_ref=tok.at[half, pl.ds(0, size)],
                        dst_ref=tok.at[half, pl.ds(o * size, size)],
                        send_sem=ts.at[half, base + o - 1],
                        recv_sem=tr.at[half, base + o - 1],
                        device_id=member(chains[half][level], o),
                        device_id_type=MESH,
                    )
                )
        return copies

    def held(level):
        return [half_own * math.prod(g[2] for g in chain[:level]) for chain in chains]

    state = {"at": 0}

    def start_stage(level):
        for copy in stage_copies(level):
            copy.start()

    def advance():
        level = state["at"]
        if level < 4:
            for copy in stage_copies(level):
                copy.wait()
            if level < 3:
                start_stage(level + 1)
            state["at"] = level + 1

    start_stage(0)

    def remote(src, dst, at, device):
        return pltpu.make_async_remote_copy(
            src_ref=src,
            dst_ref=dst,
            send_sem=hs.at[at],
            recv_sem=hr.at[at],
            device_id=device,
            device_id_type=MESH,
        )

    to_down = remote(fine_hbm.at[pl.ds(pairs - 1, 1)], halo.at[pl.ds(0, 1)], 0, (down, lat))
    to_up = remote(fine_hbm.at[pl.ds(0, 1)], halo.at[pl.ds(1, 1)], 1, (up, lat))
    to_down.start()
    to_up.start()

    local[0].wait()
    cols_s[0] = fine[:, :, 0:16, :].astype(F32)[:, :, 0:1, :]
    cols_s[1] = fine[:, :, width - 16 : width, :].astype(F32)[:, :, 15:16, :]
    side_copies = []
    for side, (there, ok_send) in enumerate(((west, has_west), (east, has_east))):
        got = cols_r.at[1 - side]
        mine = cols_s.at[side]
        side_copies.append(
            [
                remote(mine, got.at[pl.ds(1, pairs)], 2 + side * 3, (lon, there)),
                remote(
                    mine.at[pl.ds(pairs - 1, 1)],
                    got.at[pl.ds(0, 1)],
                    3 + side * 3,
                    (down, there),
                ),
                remote(
                    mine.at[pl.ds(0, 1)],
                    got.at[pl.ds(pairs + 1, 1)],
                    4 + side * 3,
                    (up, there),
                ),
            ]
        )

    def start_side(side):
        for copy in side_copies[side]:
            copy.start()

    pl.when(has_west)(lambda: start_side(0))
    pl.when(has_east)(lambda: start_side(1))

    gain0 = norm_gains[0:1, :]
    gain1 = norm_gains[1:2, :]
    n0 = chunk_of(pairs, 4)

    def put(dst, at, n, q, v, slot):
        base = q * 3 * ch
        room = hb.at[slot]
        room[0:n, q, LEFT : LEFT + width, :] = v
        dst[pl.ds(at, n), :, base + ch : base + 2 * ch] = v.astype(BF16)
        for b in (0, 2):
            lo = LEFT - 1 + b
            col = base + b * ch
            dst[pl.ds(at, n), :, col : col + ch] = room[0:n, q, lo : lo + width, :].astype(BF16)

    def patch(dst, cols):
        row = lax.broadcasted_iota(jnp.int32, (1, 16, ch), 1)
        for q in range(2):
            for side, lo, at in ((0, 0, 0), (1, width - 16, 15)):
                col = (q * 3 + 2 * side) * ch
                old = dst[:, lo : lo + 16, col : col + ch].astype(F32)
                new = jnp.where(row == at, cols[side][:, q], old)
                dst[:, lo : lo + 16, col : col + ch] = new.astype(BF16)

    def first(i, c):
        at = pl.multiple_of(i * n0, n0)
        v = norm_silu(fine[pl.ds(at, n0)].astype(F32), ones, gain0)
        for q in range(2):
            put(x1, at + 1, n0, q, v[:, q], q)
        return c

    lax.fori_loop(0, pairs // n0, first, 0)

    to_down.wait()
    to_up.wait()
    v = norm_silu(halo[...].astype(F32), ones, gain0)
    for q in range(2):
        put(x1, 0, 1, q, v[0:1, q], 0)
        put(x1, pairs + 1, 1, q, v[1:2, q], 1)

    def wait_send(side):
        for copy in side_copies[side]:
            copy.wait_send()

    def wait_recv(side):
        for copy in side_copies[side]:
            copy.wait_recv()

    pl.when(has_west)(lambda: wait_send(0))
    pl.when(has_east)(lambda: wait_send(1))
    pl.when(has_east)(lambda: wait_recv(0))
    pl.when(has_west)(lambda: wait_recv(1))
    gain0c = gain0.reshape(1, 1, 1, ch)
    sides = []
    for side in range(2):
        v = cols_r[side]
        ms = jnp.mean(v * v, axis=-1, keepdims=True)
        sides.append(silu(v * lax.rsqrt(ms + 1e-6) * gain0c))
    patch(x1, sides)
    advance()
    for copy in taps:
        copy.wait()

    half_k = 6 * ch

    def conv(x, at, n, conv_at):
        wa = w[conv_at, 0:2].reshape(half_k, 2 * ch)
        wb = w[conv_at, 2:4].reshape(half_k, 2 * ch)
        a = x[pl.ds(at, n)].reshape(n * width, half_k)
        b = x[pl.ds(at + 1, n)].reshape(n * width, half_k)
        return mm(a, wa) + mm(b, wb)

    n1 = chunk_of(pairs + 1, 13)

    def second(i, c):
        at = i * n1
        parts = ((0, (n1 + 1) // 2), ((n1 + 1) // 2, n1))
        results = [conv(x1, at + lo, hi - lo, 0) for lo, hi in parts]
        for slot, (lo, hi) in enumerate(parts):
            y, n = results[slot], hi - lo
            ms = mm((y * y).astype(BF16), ones2)
            z = y * lax.rsqrt(ms + 1e-6)
            for q in range(2):
                v = silu(z[:, q * ch : (q + 1) * ch] * gain1).reshape(n, width, ch)
                put(x2, at + lo, n, q, v, slot)
                cols2_s[0, pl.ds(at + lo, n), q] = v[:, 0:1]
                cols2_s[1, pl.ds(at + lo, n), q] = v[:, width - 1 : width]
        return c

    loops = (pairs + 1) // n1
    lax.fori_loop(0, (loops + 1) // 2, second, 0)
    advance()
    lax.fori_loop((loops + 1) // 2, loops, second, 0)

    def remote2(side, there):
        return pltpu.make_async_remote_copy(
            src_ref=cols2_s.at[side],
            dst_ref=cols2_r.at[1 - side],
            send_sem=c2s.at[side],
            recv_sem=c2r.at[side],
            device_id=(lon, there),
            device_id_type=MESH,
        )

    to_west, to_east = remote2(0, west), remote2(1, east)
    pl.when(has_west)(to_west.start)
    pl.when(has_east)(to_east.start)

    for copy in local[1:]:
        copy.wait()
    heads = wide // head_gains.shape[1]
    hd = wide // heads
    tg = token_gain[...]
    gq = jnp.concatenate([head_gains[0:1, :]] * heads, axis=1)
    gk = jnp.concatenate([head_gains[1:2, :]] * heads, axis=1)
    per_head = block_ones(wide, hd, 1.0 / hd)

    def norm_tokens(t):
        return (t * lax.rsqrt(jnp.mean(t * t, axis=-1, keepdims=True) + 1e-6) * tg).astype(BF16)

    def norm_heads(v, g):
        return v * lax.rsqrt(mm((v * v).astype(BF16), per_head) + 1e-6) * g

    mine = stage[...]
    q = norm_heads(mm(norm_tokens(mine), wq[...]), gq) * (1.0 / math.sqrt(hd))
    r = lax.broadcasted_iota(jnp.int32, (heads * own, wide), 0) // own
    c = lax.broadcasted_iota(jnp.int32, (heads * own, wide), 1) // hd
    head_mask = r == c
    qb = jnp.where(head_mask, jnp.concatenate([q] * heads, axis=0), 0.0).astype(BF16)

    def attend(nt, i, carry):
        acc, tot = carry
        t = tok[:, pl.ds(pl.multiple_of(i * nt, nt), nt)].reshape(2 * nt, wide).astype(F32)
        kv = mm(norm_tokens(t), wkv[...])
        k = norm_heads(kv[:, :wide], gk).astype(BF16)
        vv = kv[:, wide:].astype(BF16)
        s = lax.dot_general(qb, k, (((1,), (1,)), ((), ())), preferred_element_type=F32)
        e = jnp.exp(s)
        return acc + mm(e.astype(BF16), vv), tot + jnp.sum(e, axis=1, keepdims=True)

    carry = (jnp.zeros((heads * own, wide), F32), jnp.zeros((heads * own, 1), F32))
    done = 0
    while True:
        ready = min(held(state["at"]))
        if ready - done >= 128:
            nt = math.gcd(ready - done, 256)
            nt = math.gcd(nt, done) if done else nt
            carry = lax.fori_loop(done // nt, ready // nt, functools.partial(attend, nt), carry)
            done = ready
        if state["at"] == 4:
            break
        advance()
    acc, tot = carry
    att = jnp.where(head_mask, acc / tot, 0.0).reshape(heads, own, wide)
    att = jnp.sum(att, axis=0).astype(BF16)
    coarse = (mine + mm(att, wo[...])).astype(BF16)
    stage[...] = coarse.astype(F32)
    for i in range(lon_t):
        coarse_out[i] = stage[i * lat_t : (i + 1) * lat_t].astype(BF16)
    rr = lax.broadcasted_iota(jnp.int32, (lon_t * width, own), 0) // (width // lat_t)
    cc = lax.broadcasted_iota(jnp.int32, (lon_t * width, own), 1)
    rep = mm(jnp.where(rr == cc, 1.0, 0.0).astype(BF16), coarse).astype(BF16)
    lift[...] = mm(rep, we[...]).reshape(lon_t, width, ch)

    pl.when(has_west)(to_west.wait_send)
    pl.when(has_east)(to_east.wait_send)
    pl.when(has_east)(to_west.wait_recv)
    pl.when(has_west)(to_east.wait_recv)
    patch(x2, cols2_r)
    n2 = pairs // lon_t

    def out_copy(i):
        at = pl.multiple_of(i * n2, n2)
        return pltpu.make_async_copy(
            outs.at[pl.ds(at, n2)], out_hbm.at[pl.ds(at, n2)], osem.at[i]
        )

    def third(i, c):
        results = [conv(x2, pl.multiple_of((2 * i + k) * n2, n2), n2, 1) for k in range(2)]
        for k in range(2):
            at = pl.multiple_of((2 * i + k) * n2, n2)
            y = results[k]
            up_row = lift[2 * i + k]
            for q in range(2):
                v = y[:, q * ch : (q + 1) * ch].reshape(n2, width, ch)
                outs[pl.ds(at, n2), q] = (
                    fine[pl.ds(at, n2), q].astype(F32) + v + up_row[None]
                ).astype(BF16)
            out_copy(2 * i + k).start()
        return c

    lax.fori_loop(0, lon_t // 2, third, 0)
    for i in range(lon_t):
        out_copy(i).wait()


def hand_on(fine_in, coarse_in, fine_out, coarse_out, sems):
    parts = sems.shape[0] - 1
    n = fine_in.shape[0] // parts
    copies = [pltpu.make_async_copy(coarse_in, coarse_out, sems.at[parts])]
    for i in range(parts):
        part = pl.ds(i * n, n)
        copies.append(pltpu.make_async_copy(fine_in.at[part], fine_out.at[part], sems.at[i]))
    for copy in copies:
        copy.start()
    for copy in copies:
        copy.wait()


def local(lon_n, lat_n, fine_state, coarse_state, norm_gains, kernels, token_gain, head_gains,
          query_weight, keyvalue_weight, output_weight, expand_weight):
    rows, width, ch = fine_state.shape
    lon_t, lat_t, wide = coarse_state.shape
    pairs, own = rows // 2, lon_t * lat_t
    hops = lat_n // 2 + lon_n // 2
    tokens = own * lon_n * lat_n
    vm = pl.BlockSpec(memory_space=pltpu.VMEM)
    hbm = pl.BlockSpec(memory_space=pltpu.HBM)
    sem = pltpu.SemaphoreType.DMA
    fine_result, coarse_result = pl.pallas_call(
        functools.partial(body, lon_n, lat_n),
        out_shape=(
            jax.ShapeDtypeStruct((pairs, 2, width, ch), BF16),
            jax.ShapeDtypeStruct(coarse_state.shape, BF16),
        ),
        in_specs=[hbm, vm, vm, hbm, vm, vm, hbm, hbm, hbm, hbm],
        out_specs=(hbm, vm),
        scratch_shapes=[
            pltpu.VMEM((pairs, 2, width, ch), BF16),
            pltpu.VMEM((pairs, 2, width, ch), BF16),
            pltpu.VMEM(query_weight.shape, BF16),
            pltpu.VMEM(keyvalue_weight.shape, BF16),
            pltpu.VMEM(output_weight.shape, BF16),
            pltpu.VMEM(expand_weight.shape, BF16),
            pltpu.VMEM((2, 7, 2, width + 16, ch), F32),
            pltpu.VMEM((pairs + 2, width, 6 * ch), BF16),
            pltpu.VMEM((pairs + 1, width, 6 * ch), BF16),
            pltpu.VMEM((own, wide), F32),
            pltpu.VMEM((2, 4, 3, ch, 2 * ch), BF16),
            pltpu.VMEM((2, tokens // 2, wide), BF16),
            pltpu.VMEM((lon_t, width, ch), F32),
            pltpu.VMEM((2, 2, width, ch), BF16),
            pltpu.VMEM((2, pairs, 2, 1, ch), F32),
            pltpu.VMEM((2, pairs + 2, 2, 1, ch), F32),
            pltpu.VMEM((2, pairs + 1, 2, 1, ch), F32),
            pltpu.VMEM((2, pairs + 1, 2, 1, ch), F32),
            sem((5,)),
            sem((12,)),
            sem((lon_t,)),
            sem((8,)),
            sem((8,)),
            sem((2,)),
            sem((2,)),
            sem((2, hops)),
            sem((2, hops)),
        ],
        compiler_params=pltpu.CompilerParams(
            collective_id=0, has_side_effects=True, vmem_limit_bytes=56 * 2**20
        ),
    )(
        fine_state.reshape(pairs, 2, width, ch),
        coarse_state,
        norm_gains,
        kernels,
        token_gain.reshape(1, wide),
        head_gains,
        query_weight,
        keyvalue_weight,
        output_weight,
        expand_weight,
    )
    anywhere = pl.BlockSpec(memory_space=pl.ANY)
    fine_result, coarse_result = pl.pallas_call(
        hand_on,
        out_shape=(
            jax.ShapeDtypeStruct(fine_result.shape, BF16),
            jax.ShapeDtypeStruct(coarse_result.shape, BF16),
        ),
        in_specs=[anywhere] * 2,
        out_specs=(anywhere,) * 2,
        scratch_shapes=[sem((lon_t + 1,))],
        compiler_params=pltpu.CompilerParams(vmem_limit_bytes=60 * 2**20),
    )(fine_result, coarse_result)
    return fine_result.reshape(fine_state.shape), coarse_result


def solution(mesh):
    split = P("lon", "lat", None)
    return jax.shard_map(
        functools.partial(local, mesh.shape["lon"], mesh.shape["lat"]),
        mesh=mesh,
        in_specs=(split, split) + (P(),) * 8,
        out_specs=(split, split),
        check_vma=False,
    )
```

```python
import functools
import math

import jax
import jax.numpy as jnp
from jax import lax
from jax.experimental import pallas as pl
from jax.experimental.pallas import tpu as pltpu
from jax.sharding import PartitionSpec as P

MESH = pl.DeviceIdType.MESH
F32 = jnp.float32
BF16 = jnp.bfloat16
LEFT = 8


def mm(a, b):
    return jnp.dot(a, b, preferred_element_type=F32)


def block_ones(size, block, value):
    r = lax.broadcasted_iota(jnp.int32, (size, size), 0) // block
    c = lax.broadcasted_iota(jnp.int32, (size, size), 1) // block
    return jnp.where(r == c, value, 0.0).astype(BF16)


def silu(v):
    half = 0.5 * v
    return half + half * jnp.tanh(half)


def norm_silu(x, ones, gain):
    flat = x.reshape(-1, x.shape[-1])
    ms = mm((flat * flat).astype(BF16), ones)
    return silu(flat * lax.rsqrt(ms + 1e-6) * gain).reshape(x.shape)


def chunk_of(total, most):
    return max(d for d in range(1, most + 1) if total % d == 0)


def body(
    lon_n,
    lat_n,
    fine_hbm,
    coarse_in,
    norm_gains,
    kernels,
    token_gain,
    head_gains,
    wq_hbm,
    wkv_hbm,
    wo_hbm,
    we_hbm,
    out_hbm,
    coarse_out,
    outs,
    fine,
    wq,
    wkv,
    wo,
    we,
    hb,
    x1,
    x2,
    stage,
    w,
    tok,
    lift,
    halo,
    cols_s,
    cols_r,
    cols2_s,
    cols2_r,
    dma,
    wsem,
    osem,
    hs,
    hr,
    c2s,
    c2r,
    ts,
    tr,
):
    pairs, _, width, ch = fine.shape
    rows = 2 * pairs
    lon_t, lat_t, wide = coarse_in.shape
    own = lon_t * lat_t
    lon, lat = lax.axis_index("lon"), lax.axis_index("lat")
    up, down = lax.rem(lon + lon_n - 1, lon_n), lax.rem(lon + 1, lon_n)
    west, east = lax.rem(lat + lat_n - 1, lat_n), lax.rem(lat + 1, lat_n)
    has_west, has_east = lat > 0, lat < lat_n - 1

    by_z = ("lat", 2, lat_n // 2)
    by_x = ("lat", 1, 2)
    by_y = ("lon", 2, lon_n // 2)
    by_core = ("lon", 1, 2)
    chains = ((by_z, by_x, by_y, by_core), (by_z, by_y, by_x, by_core))

    def member(stage_at, offset):
        axis, stride, group = stage_at
        index = lon if axis == "lon" else lat
        place = (index // stride) % group
        moved = index + ((place + offset) % group - place) * stride
        return (moved, lat) if axis == "lon" else (lon, moved)

    partners = [member(stage_at, o) for stage_at in chains[0] for o in range(1, stage_at[2])]

    taps = []
    for conv in range(2):
        for r in range(2):
            for a in range(3):
                taps.append(
                    pltpu.make_async_copy(
                        kernels.at[conv, a],
                        w.at[conv, a + r, :, :, pl.ds(r * ch, ch)],
                        wsem.at[len(taps)],
                    )
                )
    local = [
        pltpu.make_async_copy(src, dst, dma.at[i])
        for i, (src, dst) in enumerate(
            ((fine_hbm, fine), (wq_hbm, wq), (wkv_hbm, wkv), (wo_hbm, wo), (we_hbm, we))
        )
    ]
    for copy in local[:1] + taps + local[1:]:
        copy.start()

    cols_r[...] = jnp.zeros_like(cols_r)
    cols2_r[...] = jnp.zeros_like(cols2_r)
    hb[...] = jnp.zeros_like(hb)
    barrier = pltpu.get_barrier_semaphore()
    ring = [(i, j) for i in (up, lon, down) for j in (west, lat, east)]
    del ring[4]
    for device in ring + partners:
        pl.semaphore_signal(barrier, inc=1, device_id=device, device_id_type=MESH)

    for i in range(lon_t):
        stage[i * lat_t : (i + 1) * lat_t] = coarse_in[i].astype(F32)
    half_own = own // 2
    for half in range(2):
        tok[half, 0:half_own] = stage[half * half_own : (half + 1) * half_own].astype(BF16)
    zero = jnp.zeros((3, ch, ch), BF16)
    for conv in range(2):
        w[conv, 3, :, :, pl.ds(0, ch)] = zero
        w[conv, 0, :, :, pl.ds(ch, ch)] = zero
    ones = block_ones(ch, ch, 1.0 / ch)
    ones2 = block_ones(2 * ch, ch, 1.0 / ch)

    pl.semaphore_wait(barrier, len(ring) + len(partners))

    def stage_copies(level):
        copies = []
        for half in range(2):
            size, base = half_own, 0
            for done_stage in chains[half][:level]:
                size *= done_stage[2]
                base += done_stage[2] - 1
            for o in range(1, chains[half][level][2]):
                copies.append(
                    pltpu.make_async_remote_copy(
                        src_ref=tok.at[half, pl.ds(0, size)],
                        dst_ref=tok.at[half, pl.ds(o * size, size)],
                        send_sem=ts.at[half, base + o - 1],
                        recv_sem=tr.at[half, base + o - 1],
                        device_id=member(chains[half][level], o),
                        device_id_type=MESH,
                    )
                )
        return copies

    def held(level):
        return [half_own * math.prod(g[2] for g in chain[:level]) for chain in chains]

    state = {"at": 0}

    def start_stage(level):
        for copy in stage_copies(level):
            copy.start()

    def advance():
        level = state["at"]
        if level < 4:
            for copy in stage_copies(level):
                copy.wait()
            if level < 3:
                start_stage(level + 1)
            state["at"] = level + 1

    start_stage(0)

    def remote(src, dst, at, device):
        return pltpu.make_async_remote_copy(
            src_ref=src,
            dst_ref=dst,
            send_sem=hs.at[at],
            recv_sem=hr.at[at],
            device_id=device,
            device_id_type=MESH,
        )

    to_down = remote(fine_hbm.at[pl.ds(pairs - 1, 1)], halo.at[pl.ds(0, 1)], 0, (down, lat))
    to_up = remote(fine_hbm.at[pl.ds(0, 1)], halo.at[pl.ds(1, 1)], 1, (up, lat))
    to_down.start()
    to_up.start()

    local[0].wait()
    cols_s[0] = fine[:, :, 0:16, :].astype(F32)[:, :, 0:1, :]
    cols_s[1] = fine[:, :, width - 16 : width, :].astype(F32)[:, :, 15:16, :]
    side_copies = []
    for side, (there, ok_send) in enumerate(((west, has_west), (east, has_east))):
        got = cols_r.at[1 - side]
        mine = cols_s.at[side]
        side_copies.append(
            [
                remote(mine, got.at[pl.ds(1, pairs)], 2 + side * 3, (lon, there)),
                remote(
                    mine.at[pl.ds(pairs - 1, 1)],
                    got.at[pl.ds(0, 1)],
                    3 + side * 3,
                    (down, there),
                ),
                remote(
                    mine.at[pl.ds(0, 1)],
                    got.at[pl.ds(pairs + 1, 1)],
                    4 + side * 3,
                    (up, there),
                ),
            ]
        )

    def start_side(side):
        for copy in side_copies[side]:
            copy.start()

    pl.when(has_west)(lambda: start_side(0))
    pl.when(has_east)(lambda: start_side(1))

    gain0 = norm_gains[0:1, :]
    gain1 = norm_gains[1:2, :]
    n0 = chunk_of(pairs, 4)

    def put(dst, at, n, q, v, slot):
        base = q * 3 * ch
        room = hb.at[slot]
        room[0:n, q, LEFT : LEFT + width, :] = v
        dst[pl.ds(at, n), :, base + ch : base + 2 * ch] = v.astype(BF16)
        for b in (0, 2):
            lo = LEFT - 1 + b
            col = base + b * ch
            dst[pl.ds(at, n), :, col : col + ch] = room[0:n, q, lo : lo + width, :].astype(BF16)

    def patch(dst, cols):
        row = lax.broadcasted_iota(jnp.int32, (1, 16, ch), 1)
        for q in range(2):
            for side, lo, at in ((0, 0, 0), (1, width - 16, 15)):
                col = (q * 3 + 2 * side) * ch
                old = dst[:, lo : lo + 16, col : col + ch].astype(F32)
                new = jnp.where(row == at, cols[side][:, q], old)
                dst[:, lo : lo + 16, col : col + ch] = new.astype(BF16)

    def first(i, c):
        at = pl.multiple_of(i * n0, n0)
        v = norm_silu(fine[pl.ds(at, n0)].astype(F32), ones, gain0)
        for q in range(2):
            put(x1, at + 1, n0, q, v[:, q], q)
        return c

    lax.fori_loop(0, pairs // n0, first, 0)

    to_down.wait()
    to_up.wait()
    v = norm_silu(halo[...].astype(F32), ones, gain0)
    for q in range(2):
        put(x1, 0, 1, q, v[0:1, q], 0)
        put(x1, pairs + 1, 1, q, v[1:2, q], 1)

    def wait_send(side):
        for copy in side_copies[side]:
            copy.wait_send()

    def wait_recv(side):
        for copy in side_copies[side]:
            copy.wait_recv()

    pl.when(has_west)(lambda: wait_send(0))
    pl.when(has_east)(lambda: wait_send(1))
    pl.when(has_east)(lambda: wait_recv(0))
    pl.when(has_west)(lambda: wait_recv(1))
    gain0c = gain0.reshape(1, 1, 1, ch)
    sides = []
    for side in range(2):
        v = cols_r[side]
        ms = jnp.mean(v * v, axis=-1, keepdims=True)
        sides.append(silu(v * lax.rsqrt(ms + 1e-6) * gain0c))
    patch(x1, sides)
    advance()
    for copy in taps:
        copy.wait()

    half_k = 6 * ch

    def conv(x, at, n, conv_at):
        wa = w[conv_at, 0:2].reshape(half_k, 2 * ch)
        wb = w[conv_at, 2:4].reshape(half_k, 2 * ch)
        a = x[pl.ds(at, n)].reshape(n * width, half_k)
        b = x[pl.ds(at + 1, n)].reshape(n * width, half_k)
        return mm(a, wa) + mm(b, wb)

    n1 = chunk_of(pairs + 1, 13)

    def second(i, c):
        at = i * n1
        parts = ((0, (n1 + 1) // 2), ((n1 + 1) // 2, n1))
        results = [conv(x1, at + lo, hi - lo, 0) for lo, hi in parts]
        for slot, (lo, hi) in enumerate(parts):
            y, n = results[slot], hi - lo
            ms = mm((y * y).astype(BF16), ones2)
            z = y * lax.rsqrt(ms + 1e-6)
            for q in range(2):
                v = silu(z[:, q * ch : (q + 1) * ch] * gain1).reshape(n, width, ch)
                put(x2, at + lo, n, q, v, slot)
                cols2_s[0, pl.ds(at + lo, n), q] = v[:, 0:1]
                cols2_s[1, pl.ds(at + lo, n), q] = v[:, width - 1 : width]
        return c

    loops = (pairs + 1) // n1
    lax.fori_loop(0, (loops + 1) // 2, second, 0)
    advance()
    lax.fori_loop((loops + 1) // 2, loops, second, 0)

    def remote2(side, there):
        return pltpu.make_async_remote_copy(
            src_ref=cols2_s.at[side],
            dst_ref=cols2_r.at[1 - side],
            send_sem=c2s.at[side],
            recv_sem=c2r.at[side],
            device_id=(lon, there),
            device_id_type=MESH,
        )

    to_west, to_east = remote2(0, west), remote2(1, east)
    pl.when(has_west)(to_west.start)
    pl.when(has_east)(to_east.start)

    for copy in local[1:]:
        copy.wait()
    heads = wide // head_gains.shape[1]
    hd = wide // heads
    tg = token_gain[...]
    gq = jnp.concatenate([head_gains[0:1, :]] * heads, axis=1)
    gk = jnp.concatenate([head_gains[1:2, :]] * heads, axis=1)
    per_head = block_ones(wide, hd, 1.0 / hd)

    def norm_tokens(t):
        return (t * lax.rsqrt(jnp.mean(t * t, axis=-1, keepdims=True) + 1e-6) * tg).astype(BF16)

    def norm_heads(v, g):
        return v * lax.rsqrt(mm((v * v).astype(BF16), per_head) + 1e-6) * g

    mine = stage[...]
    q = norm_heads(mm(norm_tokens(mine), wq[...]), gq) * (1.0 / math.sqrt(hd))
    r = lax.broadcasted_iota(jnp.int32, (heads * own, wide), 0) // own
    c = lax.broadcasted_iota(jnp.int32, (heads * own, wide), 1) // hd
    head_mask = r == c
    qb = jnp.where(head_mask, jnp.concatenate([q] * heads, axis=0), 0.0).astype(BF16)

    def attend(nt, i, carry):
        acc, tot = carry
        t = tok[:, pl.ds(pl.multiple_of(i * nt, nt), nt)].reshape(2 * nt, wide).astype(F32)
        kv = mm(norm_tokens(t), wkv[...])
        k = norm_heads(kv[:, :wide], gk).astype(BF16)
        vv = kv[:, wide:].astype(BF16)
        s = lax.dot_general(qb, k, (((1,), (1,)), ((), ())), preferred_element_type=F32)
        e = jnp.exp(s)
        return acc + mm(e.astype(BF16), vv), tot + jnp.sum(e, axis=1, keepdims=True)

    carry = (jnp.zeros((heads * own, wide), F32), jnp.zeros((heads * own, 1), F32))
    done = 0
    while True:
        ready = min(held(state["at"]))
        if ready - done >= 128:
            nt = math.gcd(ready - done, 256)
            nt = math.gcd(nt, done) if done else nt
            carry = lax.fori_loop(done // nt, ready // nt, functools.partial(attend, nt), carry)
            done = ready
        if state["at"] == 4:
            break
        advance()
    acc, tot = carry
    att = jnp.where(head_mask, acc / tot, 0.0).reshape(heads, own, wide)
    att = jnp.sum(att, axis=0).astype(BF16)
    coarse = (mine + mm(att, wo[...])).astype(BF16)
    stage[...] = coarse.astype(F32)
    for i in range(lon_t):
        coarse_out[i] = stage[i * lat_t : (i + 1) * lat_t].astype(BF16)
    rr = lax.broadcasted_iota(jnp.int32, (lon_t * width, own), 0) // (width // lat_t)
    cc = lax.broadcasted_iota(jnp.int32, (lon_t * width, own), 1)
    rep = mm(jnp.where(rr == cc, 1.0, 0.0).astype(BF16), coarse).astype(BF16)
    lift[...] = mm(rep, we[...]).reshape(lon_t, width, ch)

    pl.when(has_west)(to_west.wait_send)
    pl.when(has_east)(to_east.wait_send)
    pl.when(has_east)(to_west.wait_recv)
    pl.when(has_west)(to_east.wait_recv)
    patch(x2, cols2_r)
    n2 = pairs // lon_t

    def out_copy(i):
        at = pl.multiple_of(i * n2, n2)
        return pltpu.make_async_copy(
            outs.at[pl.ds(at, n2)], out_hbm.at[pl.ds(at, n2)], osem.at[i]
        )

    def third(i, c):
        results = [conv(x2, pl.multiple_of((2 * i + k) * n2, n2), n2, 1) for k in range(2)]
        for k in range(2):
            at = pl.multiple_of((2 * i + k) * n2, n2)
            y = results[k]
            up_row = lift[2 * i + k]
            for q in range(2):
                v = y[:, q * ch : (q + 1) * ch].reshape(n2, width, ch)
                outs[pl.ds(at, n2), q] = (
                    fine[pl.ds(at, n2), q].astype(F32) + v + up_row[None]
                ).astype(BF16)
            out_copy(2 * i + k).start()
        return c

    lax.fori_loop(0, lon_t // 2, third, 0)
    for i in range(lon_t):
        out_copy(i).wait()


def hand_on(fine_in, coarse_in, fine_out, coarse_out, fine, coarse, sems):
    parts = sems.shape[1] - 1
    n = fine.shape[0] // parts
    moves = [(coarse_in, coarse, coarse_out)]
    for i in range(parts):
        part = pl.ds(i * n, n)
        moves.append((fine_in.at[part], fine.at[part], fine_out.at[part]))
    ins = [pltpu.make_async_copy(a, b, sems.at[0, i]) for i, (a, b, c) in enumerate(moves)]
    outs = [pltpu.make_async_copy(b, c, sems.at[1, i]) for i, (a, b, c) in enumerate(moves)]
    for copy in ins:
        copy.start()
    for arrived, leaving in zip(ins, outs):
        arrived.wait()
        leaving.start()
    for copy in outs:
        copy.wait()


def local(lon_n, lat_n, fine_state, coarse_state, norm_gains, kernels, token_gain, head_gains,
          query_weight, keyvalue_weight, output_weight, expand_weight):
    rows, width, ch = fine_state.shape
    lon_t, lat_t, wide = coarse_state.shape
    pairs, own = rows // 2, lon_t * lat_t
    hops = lat_n // 2 + lon_n // 2
    tokens = own * lon_n * lat_n
    vm = pl.BlockSpec(memory_space=pltpu.VMEM)
    hbm = pl.BlockSpec(memory_space=pltpu.HBM)
    sem = pltpu.SemaphoreType.DMA
    fine_result, coarse_result = pl.pallas_call(
        functools.partial(body, lon_n, lat_n),
        out_shape=(
            jax.ShapeDtypeStruct((pairs, 2, width, ch), BF16),
            jax.ShapeDtypeStruct(coarse_state.shape, BF16),
        ),
        in_specs=[hbm, vm, vm, hbm, vm, vm, hbm, hbm, hbm, hbm],
        out_specs=(hbm, vm),
        scratch_shapes=[
            pltpu.VMEM((pairs, 2, width, ch), BF16),
            pltpu.VMEM((pairs, 2, width, ch), BF16),
            pltpu.VMEM(query_weight.shape, BF16),
            pltpu.VMEM(keyvalue_weight.shape, BF16),
            pltpu.VMEM(output_weight.shape, BF16),
            pltpu.VMEM(expand_weight.shape, BF16),
            pltpu.VMEM((2, 7, 2, width + 16, ch), F32),
            pltpu.VMEM((pairs + 2, width, 6 * ch), BF16),
            pltpu.VMEM((pairs + 1, width, 6 * ch), BF16),
            pltpu.VMEM((own, wide), F32),
            pltpu.VMEM((2, 4, 3, ch, 2 * ch), BF16),
            pltpu.VMEM((2, tokens // 2, wide), BF16),
            pltpu.VMEM((lon_t, width, ch), F32),
            pltpu.VMEM((2, 2, width, ch), BF16),
            pltpu.VMEM((2, pairs, 2, 1, ch), F32),
            pltpu.VMEM((2, pairs + 2, 2, 1, ch), F32),
            pltpu.VMEM((2, pairs + 1, 2, 1, ch), F32),
            pltpu.VMEM((2, pairs + 1, 2, 1, ch), F32),
            sem((5,)),
            sem((12,)),
            sem((lon_t,)),
            sem((8,)),
            sem((8,)),
            sem((2,)),
            sem((2,)),
            sem((2, hops)),
            sem((2, hops)),
        ],
        compiler_params=pltpu.CompilerParams(
            collective_id=0, has_side_effects=True, vmem_limit_bytes=56 * 2**20
        ),
    )(
        fine_state.reshape(pairs, 2, width, ch),
        coarse_state,
        norm_gains,
        kernels,
        token_gain.reshape(1, wide),
        head_gains,
        query_weight,
        keyvalue_weight,
        output_weight,
        expand_weight,
    )
    anywhere = pl.BlockSpec(memory_space=pl.ANY)
    fine_result, coarse_result = pl.pallas_call(
        hand_on,
        out_shape=(
            jax.ShapeDtypeStruct(fine_result.shape, BF16),
            jax.ShapeDtypeStruct(coarse_result.shape, BF16),
        ),
        in_specs=[anywhere] * 2,
        out_specs=(anywhere,) * 2,
        scratch_shapes=[
            pltpu.VMEM(fine_result.shape, BF16),
            pltpu.VMEM(coarse_result.shape, BF16),
            sem((2, lon_t + 1)),
        ],
        compiler_params=pltpu.CompilerParams(vmem_limit_bytes=60 * 2**20),
    )(fine_result, coarse_result)
    return fine_result.reshape(fine_state.shape), coarse_result


def solution(mesh):
    split = P("lon", "lat", None)
    return jax.shard_map(
        functools.partial(local, mesh.shape["lon"], mesh.shape["lat"]),
        mesh=mesh,
        in_specs=(split, split) + (P(),) * 8,
        out_specs=(split, split),
        check_vma=False,
    )
```
